32 devices in a mesh: store: 4 (over y, core), tensor: 8 (over z, x).
Axes of the slice: x: 2, y: 2, z: 4, core: 2. Of those that a mesh axis runs over, the one named last changes fastest.
Arguments:
- decoder_rows: bfloat16 [2048, 4096], P(('store', 'tensor')), may hold values from -45 to 45
- q_weight: bfloat16 [4096, 4096], P(None, 'tensor'), may hold values from -0.09375 to 0.09375
- kv_weight: bfloat16 [2, 896, 4096], P(None, None, 'tensor'), may hold values from -0.1875 to 0.1875
- out_weight: bfloat16 [4096, 4096], P('tensor'), may hold values from -0.5 to 0.5
- store_tiles: bfloat16 [2048, 128, 896], P('store', 'tensor'), may hold values from -6 to 6
- neighbour_shard: int32 [32, 2], replicated, may hold values from 0 to 3, all different within a row; in each aligned block of 8 rows (0 to 7, 8 to 15, ...) at most 6 rows name the same one
- neighbour_tile: int32 [32, 2], replicated, may hold values from 0 to 511
Outputs:
- cross: bfloat16 [2048, 4096], P(('store', 'tensor'))
The draws below stay inside these ranges and needn't reach their ends.
Inputs may be any that keep to these rules, and one draw needn't show every extreme that they name: `neighbour_shard`: each block's 2 neighbours lie in different shards; among the 8 blocks of one sequence no shard is named more than 6 times, and in some sequence one shard is named exactly 6 times.
All inputs are finite; a program needn't handle non-finite values.
Results may differ from the reference program's by a relative error of at most 0.023.
Values may be sent and summed in bfloat16 or wider, within the bound.
A program may use at most 128 MiB of HBM per device.

```python
import math
import jax
import jax.numpy as jnp
import numpy as np
from jax import lax

D = 4096
HEADS = 32
HD = 128
ENC = 896
BLOCK = 64
NTOK = 128
NEIGH = 2
TOK_DEV = 64
TILES_SH = 512
CG = 8
SPANS = 32
TOKENS = 2048
CAP = 6
TILES = 2048
N_STORE = 4
N_TENSOR = 8


def draw_decoder_rows(key, part):
    key_rows, key_cols, key_base = jax.random.split(key, 3)
    row_factor = jnp.exp(jax.random.uniform(key_rows, (TOKENS, 1), jnp.float32, math.log(0.3), math.log(3.0)))
    col_factor = jnp.exp(jax.random.uniform(key_cols, (1, D), jnp.float32, math.log(0.3), math.log(3.0)))
    base_value = jnp.clip(jax.random.normal(key_base, (TOKENS, D), jnp.float32), -5.0, 5.0)
    return (base_value * row_factor * col_factor).astype(jnp.bfloat16)


def set_ends(values, stream_key, smallest, top_value):
    dims = values.shape
    place = [jax.random.randint(jax.random.fold_in(stream_key, axis), (), 0, dims[axis]) for axis in range(len(dims))]
    values = values.at[tuple(place)].set(smallest)
    longest = dims.index(max(dims))
    place[longest] = (place[longest] + 1) % dims[longest]
    return values.at[tuple(place)].set(top_value)


def levels(stream_key, shape, cuts, least, largest):
    loudness, own = 1.0, jax.random.fold_in(stream_key, 6)
    for dim, blocks in cuts:
        heights = jnp.exp(jax.random.uniform(jax.random.fold_in(own, dim), (blocks,), jnp.float32, least / len(cuts), largest / len(cuts)))
        loudness = loudness * jnp.repeat(heights, shape[dim] // blocks).reshape([-1 if axis == dim else 1 for axis in range(len(shape))])
    return loudness


def shared_out(key, own, number, rows, amount, top, most, slope):
    order = jax.random.permutation(key, amount)
    crowded, usual = load_shares(amount, rows * top, most, slope, True), load_shares(amount, rows * top, most, slope, False)
    places = jnp.arange(amount)

    def named(tallies, rotation):
        used = int((tallies > 0).sum())
        fixed = max(1, used // 4)
        moved = fixed + (places - fixed + rotation * (used - fixed)) % max(1, amount - fixed)
        return jnp.zeros((amount,), jnp.int32).at[order[jnp.where(places < fixed, places, moved)]].set(jnp.asarray(tallies, jnp.int32))

    tallies = jnp.where(number % 4 == 0, named(crowded, number // 4), named(usual, number - number // 4 - 1))
    mixed = jax.random.permutation(jax.random.fold_in(own, 3), amount)
    giver, sink = mixed[0:amount // 2 * 2:2], mixed[1:amount // 2 * 2:2]
    room = jnp.minimum(tallies[giver] - 1, most - tallies[sink]) // 2
    room = jnp.where((giver == order[0]) | (sink == order[0]) | (tallies[sink] == 0), 0, jnp.maximum(room, 0))
    moved = jax.random.randint(jax.random.fold_in(own, 4), (amount // 2,), 0, 1 << 20) % (room + 1)
    tallies = tallies.at[giver].add(-moved).at[sink].add(moved)
    items = jnp.searchsorted(jnp.cumsum(tallies), jnp.arange(rows * top), side="right").astype(jnp.int32)
    listing = items.reshape(top, rows).T
    listing = listing[jax.random.permutation(jax.random.fold_in(own, 1), rows)]
    rotation = jax.random.randint(jax.random.fold_in(own, 2), (rows, 1), 0, top)
    return jnp.take_along_axis(listing, (jnp.arange(top)[None, :] + rotation) % top, axis=1)


def load_shares(count, total, reach, skew, full):
    weights = [(1 << 20) // math.isqrt(rank ** skew) + 1 for rank in range(1, count + 1)]
    largest = reach if full else min(reach, max(-(-total // count), total * weights[0] // sum(weights)))
    least = 1 if total - largest >= count - 1 else 0
    given, spare = [largest] + [least] * (count - 1), total - largest - least * (count - 1)
    while spare > 0:
        free = [i for i in range(1, count) if given[i] < largest] or [i for i in range(1, count) if given[i] < reach]
        mass, budget = sum([weights[i] for i in free]), spare
        for i in free:
            more = min(reach - given[i], max(1, budget * weights[i] // mass), spare)
            given[i] = given[i] + more
            spare = spare - more
    return np.array(given)


def noise(own_key, dims, scale, bound, shards=(), kind=jnp.bfloat16):
    factor_of = levels(own_key, dims, shards, -0.22, 0.18) if shards else 1.0
    values = jax.random.normal(own_key, dims, jnp.float32) * scale * factor_of
    return jnp.minimum(jnp.maximum(values, -bound), bound).astype(kind)


def setup_inputs(seed: int = 0) -> dict:
    seeds = jax.random.split(jax.random.key(seed), 8)
    decoder_rows = draw_decoder_rows(jax.random.fold_in(seeds[7], 71), 0)
    q_weight = noise(seeds[1], (D, HEADS * HD), D ** -0.5, 0.09375, ((1, 8),))
    kv_weight = noise(seeds[2], (2, ENC, HEADS * HD), ENC ** -0.5, 0.1875, ((2, 8),))
    out_weight = noise(seeds[3], (HEADS * HD, D), HD ** -0.5, 0.5, ((0, 8),))
    store_tiles = noise(seeds[4], (TILES, NTOK, ENC), 1.0, 6.0, ((0, 4), (1, 8)))
    neighbour_shard_keys = jax.random.split(jax.random.fold_in(seeds[5], 1), SPANS // CG)
    neighbour_shard_turns = jax.random.permutation(jax.random.fold_in(seeds[5], 3), SPANS // CG)
    neighbour_shard = jax.vmap(lambda own, number: shared_out(jax.random.fold_in(seeds[5], 2), own, number, CG, N_STORE, NEIGH, CAP, 2))(neighbour_shard_keys, neighbour_shard_turns).reshape((SPANS, NEIGH))
    neighbour_tile = set_ends(jax.random.randint(seeds[6], (SPANS, NEIGH), 0, TILES_SH), jax.random.fold_in(seeds[6], 1), 0, TILES_SH - 1).astype(jnp.int32)
    return {"decoder_rows": decoder_rows, "q_weight": q_weight, "kv_weight": kv_weight, "out_weight": out_weight, "store_tiles": store_tiles, "neighbour_shard": neighbour_shard, "neighbour_tile": neighbour_tile}


def reference(decoder_rows, q_weight, kv_weight, out_weight, store_tiles, neighbour_shard, neighbour_tile):
    seq_len = TOK_DEV * N_TENSOR
    head_dev = HEADS // N_TENSOR
    q_factor = 1.0 / math.sqrt(HD)
    grouped_rows = decoder_rows.reshape(N_STORE, seq_len, D)
    grouped_shard = neighbour_shard.reshape(N_STORE, CG, NEIGH)
    grouped_tile = neighbour_tile.reshape(N_STORE, CG, NEIGH)
    part_weight = out_weight.reshape(N_TENSOR, head_dev * HD, D)

    def one_sequence(inputs):
        seq_rows, seq_shard, seq_tile = inputs
        rows_wide = seq_rows.astype(jnp.float32)
        normed = (rows_wide * lax.rsqrt(lax.optimization_barrier(jnp.mean(rows_wide * rows_wide, axis=1, keepdims=True)) + 1e-05)).astype(jnp.bfloat16)
        queries = (jnp.dot(normed, q_weight, preferred_element_type=jnp.float32) * q_factor).astype(jnp.bfloat16)
        flat_index = (seq_shard * TILES_SH + seq_tile).reshape(-1).astype(jnp.int32)
        neighbours = jnp.take(store_tiles, flat_index, axis=0)
        keys_values = jnp.einsum('rne,ced->rncd', neighbours.astype(jnp.float32), kv_weight.astype(jnp.float32)).astype(jnp.bfloat16)
        keys_values = lax.optimization_barrier(keys_values)
        keyed = keys_values.reshape(CG, NEIGH * NTOK, 2, HEADS, HD).astype(jnp.float32)
        query_blocks = queries.reshape(CG, BLOCK, HEADS, HD).astype(jnp.float32)
        scores = jnp.einsum('cqhd,ckhd->chqk', query_blocks, keyed[:, :, 0])
        expo_scores = jnp.exp(scores)
        weights = (expo_scores / lax.optimization_barrier(jnp.sum(expo_scores, axis=3, keepdims=True))).astype(jnp.bfloat16)
        weights = lax.optimization_barrier(weights).astype(jnp.float32)
        attended = jnp.einsum('chqk,ckhd->cqhd', weights, keyed[:, :, 1]).astype(jnp.bfloat16)
        part_rows = attended.reshape(seq_len, N_TENSOR, head_dev * HD)

        def add_partial(head_group, running):
            rows_part = lax.dynamic_index_in_dim(part_rows, head_group, 1, keepdims=False)
            weight_part = lax.dynamic_index_in_dim(part_weight, head_group, 0, keepdims=False)
            partial_term = jnp.dot(rows_part, weight_part, preferred_element_type=jnp.float32).astype(jnp.bfloat16)
            partial_term = lax.optimization_barrier(partial_term)
            return running + partial_term.astype(jnp.float32)
        summed = lax.fori_loop(0, N_TENSOR, add_partial, jnp.zeros((seq_len, D), jnp.float32))
        return summed.astype(jnp.bfloat16)
    result = lax.map(one_sequence, (grouped_rows, grouped_shard, grouped_tile))
    return result.reshape(TOKENS, D)
```

```python
import functools
import math

import jax
import jax.numpy as jnp
from jax import lax
from jax.experimental import pallas as pl
from jax.experimental.pallas import tpu as pltpu
from jax.sharding import PartitionSpec as P

HD = 128
BLOCK = 64
NTOK = 128
NEIGH = 2
LINE = 4
F32 = jnp.float32
BF16 = jnp.bfloat16
MESH = pl.DeviceIdType.MESH


def pick_kernel(
    store_count, request_count, capacity, shard_ref, tile_ref, tiles_ref, out_ref, slot_ref,
    table, count, sem,
):
    me = lax.axis_index("store")
    slots = store_count * capacity

    @pl.loop(0, slots)
    def _(i):
        table[i] = 0

    for s in range(store_count):
        count[s] = 0

        def step(r, c, s=s):
            hit = shard_ref[s * request_count + r] == me
            table[jnp.where(hit, s * capacity + c, slots)] = tile_ref[s * request_count + r]
            return c + hit.astype(jnp.int32)

        lax.fori_loop(0, request_count, step, jnp.int32(0))

    @pl.loop(0, slots)
    def _(i):
        pltpu.make_async_copy(tiles_ref.at[table[i]], out_ref.at[i], sem).start()

    @pl.loop(0, request_count)
    def _(r):
        shard = shard_ref[me * request_count + r]
        slot_ref[r] = shard * capacity + count[shard]
        count[shard] = count[shard] + 1

    pltpu.make_async_copy(tiles_ref.at[pl.ds(0, slots)], out_ref, sem).wait()


def main_kernel(
    store_count, capacity, requests,
    slot_ref, dec_ref, qw_hbm, kvw_hbm, ow_hbm, outgoing, out_ref,
    rows, neigh, arrived, qw, kvw, ow, q_buf, k_buf, v_buf, att, part, xrecv, up, down,
    load_sem, a2a_send, a2a_recv, rows_send, rows_recv, neigh_send, neigh_recv,
    part_send, part_recv, chain_send, up_recv, down_recv,
):
    store = lax.axis_index("store")
    tensor = lax.axis_index("tensor")
    z = lax.div(tensor, 2)
    x = lax.rem(tensor, 2)
    top = LINE - 1
    partner = z * 2 + 1 - x
    q_factor = 1.0 / math.sqrt(HD)
    head_count = qw.shape[1] // HD
    tile_rows = arrived.shape[1]

    loads = [
        pltpu.make_async_copy(src, dst, load_sem.at[i])
        for i, (src, dst) in enumerate(((kvw_hbm, kvw), (qw_hbm, qw), (ow_hbm, ow)))
    ]
    own_slots = pl.ds(store * capacity, capacity)
    own_tiles = pltpu.make_async_copy(
        outgoing.at[own_slots], arrived.at[own_slots], load_sem.at[3]
    )
    own_tiles.start()
    for load in loads:
        load.start()

    barrier = pltpu.get_barrier_semaphore()
    for k in range(1, store_count):
        peer = lax.rem(store + k, store_count)
        pl.semaphore_signal(barrier, inc=1, device_id=(peer, tensor), device_id_type=MESH)
    pl.semaphore_signal(barrier, inc=1, device_id=(store, partner), device_id_type=MESH)

    @pl.when(z > 0)
    def _():
        pl.semaphore_signal(barrier, inc=1, device_id=(store, tensor - 2), device_id_type=MESH)

    @pl.when(z < top)
    def _():
        pl.semaphore_signal(barrier, inc=1, device_id=(store, tensor + 2), device_id_type=MESH)

    inner = (z > 0) & (z < top)

    @pl.when(inner)
    def _():
        pl.semaphore_wait(barrier, store_count + 2)

    @pl.when(jnp.logical_not(inner))
    def _():
        pl.semaphore_wait(barrier, store_count + 1)

    def tiles_copy(k):
        peer = lax.rem(store + k, store_count)
        return pltpu.make_async_remote_copy(
            src_ref=outgoing.at[pl.ds(peer * capacity, capacity)],
            dst_ref=arrived.at[own_slots],
            send_sem=a2a_send.at[k - 1],
            recv_sem=a2a_recv.at[k - 1],
            device_id=(peer, tensor),
            device_id_type=MESH,
        )

    for k in range(1, store_count):
        tiles_copy(k).start()

    def block_copy(buf, send, recv, way, j):
        target = (tensor + 2, tensor - 2, partner)[way]
        return pltpu.make_async_remote_copy(
            src_ref=buf.at[j],
            dst_ref=buf.at[j],
            send_sem=send.at[way, j],
            recv_sem=recv.at[j],
            device_id=(store, target),
            device_id_type=MESH,
        )

    row_copy = functools.partial(block_copy, rows, rows_send, rows_recv)
    neigh_copy = functools.partial(block_copy, neigh, neigh_send, neigh_recv)

    def send_own(copy):
        @pl.when(z < top)
        def _():
            copy(0, tensor).start()

        @pl.when(z > 0)
        def _():
            copy(1, tensor).start()

        copy(2, tensor).start()

    def forward(copy, d):
        @pl.when(z - d >= 0)
        def _():
            j = tensor - 2 * d
            copy(0, j).wait_recv()

            @pl.when(z < top)
            def _():
                copy(0, j).start()

            copy(2, j).start()

        @pl.when(z + d <= top)
        def _():
            j = tensor + 2 * d
            copy(1, j).wait_recv()

            @pl.when(z > 0)
            def _():
                copy(1, j).start()

            copy(2, j).start()

    @pl.loop(0, dec_ref.shape[0] // 16)
    def _(i):
        at = pl.ds(pl.multiple_of(i * 16, 16), 16)
        wide = dec_ref[at, :].astype(F32)
        scale = lax.rsqrt(jnp.mean(wide * wide, axis=1, keepdims=True) + 1e-05)
        rows[tensor, at, :] = (wide * scale).astype(BF16)

    send_own(row_copy)

    own_tiles.wait()
    for k in range(1, store_count):
        tiles_copy(k).wait_recv()

    @pl.loop(0, requests)
    def _(r):
        picked = arrived[slot_ref[r]]
        neigh[tensor, pl.ds(pl.multiple_of(r * tile_rows, tile_rows), tile_rows), :] = picked

    send_own(neigh_copy)

    def project(j):
        source = neigh[j]
        for a, dst in ((0, k_buf), (1, v_buf)):
            got = jnp.dot(source, kvw[a], preferred_element_type=F32).astype(BF16)
            dst[j] = got.reshape(dst.shape[1:])

    loads[0].wait()
    project(tensor)

    @pl.loop(1, LINE)
    def _(d):
        forward(row_copy, d)
        forward(neigh_copy, d)

        @pl.when(z - d >= 0)
        def _():
            project(tensor - 2 * d)

        @pl.when(z + d <= top)
        def _():
            project(tensor + 2 * d)

    for p in range(LINE):
        row_copy(2, p * 2 + 1 - x).wait_recv()
    loads[1].wait()

    @pl.loop(0, qw.shape[1] // 256)
    def _(c):
        at = pl.ds(pl.multiple_of(c * 256, 256), 256)
        all_rows = rows[...].reshape(-1, rows.shape[2])
        got = jnp.dot(all_rows, qw[:, at], preferred_element_type=F32)
        q_buf[:, :, at] = (got * q_factor).astype(BF16).reshape(q_buf.shape[0], BLOCK, 256)

    half = lax.div(z, 2)
    near = z + half * (3 - 2 * z)

    def place(k):
        o = (3, 2 - 2 * near, 1 + near, near)[k]
        return o + half * (3 - 2 * o)

    for k in reversed(range(LINE)):
        j = place(k) * 2 + 1 - x
        neigh_copy(2, j).wait_recv()
        project(j)
    loads[2].wait()

    def part_copy(p):
        return pltpu.make_async_remote_copy(
            src_ref=part.at[p, 1 - x],
            dst_ref=xrecv.at[p],
            send_sem=part_send.at[p],
            recv_sem=part_recv.at[p],
            device_id=(store, partner),
            device_id_type=MESH,
        )

    def chain_copy(way, p):
        return pltpu.make_async_remote_copy(
            src_ref=part.at[p, x],
            dst_ref=(up, down)[way].at[p],
            send_sem=chain_send.at[p],
            recv_sem=(up_recv, down_recv)[way].at[p],
            device_id=(store, (tensor + 2, tensor - 2)[way]),
            device_id_type=MESH,
        )

    def attend(p):
        @pl.loop(0, 2)
        def _(i):
            b = p * 2 + i
            for h in range(head_count):
                cols = slice(h * HD, (h + 1) * HD)
                keys = k_buf[:, b, :, cols].reshape(-1, HD)
                values = v_buf[:, b, :, cols].reshape(-1, HD)
                scores = lax.dot_general(
                    q_buf[b, :, cols], keys, (((1,), (1,)), ((), ())),
                    preferred_element_type=F32,
                )
                expo = jnp.exp(scores)
                weights = (expo / jnp.sum(expo, axis=1, keepdims=True)).astype(BF16)
                got = jnp.dot(weights, values, preferred_element_type=F32)
                att[i, :, cols] = got.astype(BF16)

        @pl.loop(0, ow.shape[1] // 512)
        def _(c):
            at = pl.ds(pl.multiple_of(c * 512, 512), 512)
            both = att[...].reshape(-1, att.shape[2])
            got = jnp.dot(both, ow[:, at], preferred_element_type=F32).astype(BF16)
            part[p, :, :, at] = got.reshape(2, BLOCK, 512)

        part_copy(p).start()

    def add(p, *terms):
        @pl.loop(0, BLOCK // 16)
        def _(i):
            at = pl.ds(pl.multiple_of(i * 16, 16), 16)
            total = part[p, x, at, :].astype(F32)
            for term in terms:
                total = total + term[p, at, :].astype(F32)
            part[p, x, at, :] = total.astype(BF16)

    def pass_on(p):
        part_copy(p).wait_recv()
        add(p, xrecv)

        @pl.when(p > z)
        def _():
            @pl.when(z > 0)
            def _():
                chain_copy(0, p).wait_recv()
                add(p, up)

            chain_copy(0, p).start()

        @pl.when(p < z)
        def _():
            @pl.when(z < top)
            def _():
                chain_copy(1, p).wait_recv()
                add(p, down)

            chain_copy(1, p).start()

    attend(place(0))
    attend(place(1))
    pass_on(place(0))
    attend(place(2))
    pass_on(place(1))
    attend(place(3))
    pass_on(place(2))
    part_copy(z).wait_recv()
    add(z, xrecv)

    @pl.when(z > 0)
    def _():
        chain_copy(0, z).wait_recv()
        add(z, up)

    @pl.when(z < top)
    def _():
        chain_copy(1, z).wait_recv()
        add(z, down)

    out_ref[...] = part[z, x]

    for k in range(1, store_count):
        tiles_copy(k).wait_send()
    for copy in (row_copy, neigh_copy):
        for p in range(LINE):
            j = p * 2 + x

            @pl.when((p <= z) & (z < top))
            def _():
                copy(0, j).wait_send()

            @pl.when((p >= z) & (z > 0))
            def _():
                copy(1, j).wait_send()

            copy(2, j).wait_send()
    for p in range(LINE):
        part_copy(p).wait_send()

        @pl.when(z != p)
        def _():
            chain_copy(0, p).wait_send()


def kernel_body(
    decoder_rows, q_weight, kv_weight, out_weight, store_tiles, neighbour_shard, neighbour_tile
):
    tensor_count = lax.axis_size("tensor")
    store_count = lax.axis_size("store")
    local_rows, width = decoder_rows.shape
    blocks = tensor_count * local_rows // BLOCK
    requests = blocks * NEIGH
    capacity = 3 * requests // (2 * store_count)
    slots = store_count * capacity
    tile_rows, enc = store_tiles.shape[1:]
    head_cols = q_weight.shape[1]
    hbm = pl.BlockSpec(memory_space=pl.ANY)
    smem = pl.BlockSpec(memory_space=pltpu.SMEM)
    vmem = pl.BlockSpec(memory_space=pltpu.VMEM)
    outgoing, slot_index = pl.pallas_call(
        functools.partial(pick_kernel, store_count, requests, capacity),
        out_shape=(
            jax.ShapeDtypeStruct((slots, tile_rows, enc), BF16),
            jax.ShapeDtypeStruct((requests,), jnp.int32),
        ),
        in_specs=[smem, smem, hbm],
        out_specs=(hbm, smem),
        scratch_shapes=[
            pltpu.SMEM((slots + 1,), jnp.int32),
            pltpu.SMEM((store_count,), jnp.int32),
            pltpu.SemaphoreType.DMA,
        ],
    )(neighbour_shard.reshape(-1), neighbour_tile.reshape(-1), store_tiles)
    dma = pltpu.SemaphoreType.DMA
    block_keys = NEIGH * tile_rows
    return pl.pallas_call(
        functools.partial(main_kernel, store_count, capacity, requests),
        out_shape=jax.ShapeDtypeStruct((local_rows, width), BF16),
        in_specs=[smem, vmem, hbm, hbm, hbm, hbm],
        out_specs=vmem,
        scratch_shapes=[
            pltpu.VMEM((tensor_count, local_rows, width), BF16),
            pltpu.VMEM((tensor_count, requests * tile_rows, enc), BF16),
            pltpu.VMEM((slots, tile_rows, enc), BF16),
            pltpu.VMEM(q_weight.shape, BF16),
            pltpu.VMEM(kv_weight.shape, BF16),
            pltpu.VMEM(out_weight.shape, BF16),
            pltpu.VMEM((blocks, BLOCK, head_cols), BF16),
            pltpu.VMEM((tensor_count, blocks, block_keys, head_cols), BF16),
            pltpu.VMEM((tensor_count, blocks, block_keys, head_cols), BF16),
            pltpu.VMEM((2, BLOCK, head_cols), BF16),
            pltpu.VMEM((LINE, 2, BLOCK, width), BF16),
            pltpu.VMEM((LINE, BLOCK, width), BF16),
            pltpu.VMEM((LINE, BLOCK, width), BF16),
            pltpu.VMEM((LINE, BLOCK, width), BF16),
            dma((4,)),
            dma((store_count - 1,)),
            dma((store_count - 1,)),
            dma((3, tensor_count)),
            dma((tensor_count,)),
            dma((3, tensor_count)),
            dma((tensor_count,)),
            dma((LINE,)),
            dma((LINE,)),
            dma((LINE,)),
            dma((LINE,)),
            dma((LINE,)),
        ],
        compiler_params=pltpu.CompilerParams(
            collective_id=0, has_side_effects=True, vmem_limit_bytes=56 * 2**20
        ),
    )(slot_index, decoder_rows, q_weight, kv_weight, out_weight, outgoing)


def plain_body(
    decoder_rows, q_weight, kv_weight, out_weight, store_tiles, neighbour_shard, neighbour_tile
):
    tensor_count = lax.axis_size("tensor")
    store_count = lax.axis_size("store")
    my_sequence = lax.axis_index("store")
    local_rows = decoder_rows.shape[0]
    seq_len = local_rows * tensor_count
    block_count = seq_len // BLOCK
    request_count = block_count * NEIGH
    capacity = 3 * request_count // (2 * store_count)
    head_cols = q_weight.shape[1]
    head_count = head_cols // HD
    q_factor = 1.0 / math.sqrt(HD)
    rows_wide = decoder_rows.astype(jnp.float32)
    normed = (
        rows_wide * lax.rsqrt(jnp.mean(rows_wide * rows_wide, axis=1, keepdims=True) + 1e-05)
    ).astype(jnp.bfloat16)
    queries = (
        jnp.dot(
            lax.all_gather(normed, "tensor", axis=0, tiled=True),
            q_weight,
            preferred_element_type=jnp.float32,
        )
        * q_factor
    ).astype(jnp.bfloat16)
    shard_table = neighbour_shard.reshape(store_count, request_count)
    tile_table = neighbour_tile.reshape(store_count, request_count)
    positions = jnp.arange(request_count, dtype=jnp.int32)
    before_mask = positions[None, :] < positions[:, None]
    same_shard = shard_table[:, :, None] == shard_table[:, None, :]
    rank_table = jnp.sum((same_shard & before_mask[None]).astype(jnp.int32), axis=2)
    served_here = shard_table == my_sequence
    slot_ids = jnp.arange(capacity, dtype=jnp.int32)
    slot_match = (
        served_here[:, :, None] & (rank_table[:, :, None] == slot_ids[None, None, :])
    ).astype(jnp.int32)
    slot_tile = jnp.sum(slot_match * tile_table[:, :, None], axis=1)
    outgoing = jnp.take(store_tiles, slot_tile.reshape(-1), axis=0)
    arrived = lax.all_to_all(outgoing, "store", split_axis=0, concat_axis=0, tiled=True)
    own_shard = lax.dynamic_index_in_dim(shard_table, my_sequence, 0, keepdims=False)
    own_rank = lax.dynamic_index_in_dim(rank_table, my_sequence, 0, keepdims=False)
    slot_index = own_shard * capacity + own_rank
    picked = jnp.take(arrived, slot_index, axis=0)
    projected = jnp.einsum(
        "rne,ced->rncd",
        lax.all_gather(picked, "tensor", axis=1, tiled=True),
        kv_weight,
        preferred_element_type=jnp.float32,
    )
    keys_values = projected.astype(jnp.bfloat16)
    keyed = keys_values.reshape(block_count, NEIGH * NTOK, 2, head_count, HD)
    query_blocks = queries.reshape(block_count, BLOCK, head_count, HD)
    scores = jnp.einsum(
        "cqhd,ckhd->chqk", query_blocks, keyed[:, :, 0], preferred_element_type=jnp.float32
    )
    expo_scores = jnp.exp(scores)
    weights = (expo_scores / jnp.sum(expo_scores, axis=3, keepdims=True)).astype(jnp.bfloat16)
    attended = jnp.einsum(
        "chqk,ckhd->cqhd", weights, keyed[:, :, 1], preferred_element_type=jnp.float32
    )
    attended = attended.astype(jnp.bfloat16).reshape(seq_len, head_cols)
    return lax.psum_scatter(
        jnp.dot(attended, out_weight, preferred_element_type=jnp.float32).astype(jnp.bfloat16),
        "tensor",
        scatter_dimension=0,
        tiled=True,
    )


def body(*args):
    fits = (
        lax.axis_size("tensor") == 2 * LINE
        and args[0].shape[0] == BLOCK
        and args[4].shape[1] % 16 == 0
    )
    return (kernel_body if fits else plain_body)(*args)


def solution(mesh):
    in_specs = (
        P(("store", "tensor"), None),
        P(None, "tensor"),
        P(None, None, "tensor"),
        P("tensor", None),
        P("store", "tensor", None),
        P(),
        P(),
    )
    out_specs = P(("store", "tensor"), None)
    return jax.shard_map(body, mesh=mesh, in_specs=in_specs, out_specs=out_specs, check_vma=False)
```

```python
import functools
import math

import jax
import jax.numpy as jnp
from jax import lax
from jax.experimental import pallas as pl
from jax.experimental.pallas import tpu as pltpu
from jax.sharding import PartitionSpec as P

HD = 128
BLOCK = 64
NTOK = 128
NEIGH = 2
LINE = 4
F32 = jnp.float32
BF16 = jnp.bfloat16
MESH = pl.DeviceIdType.MESH


def main_kernel(
    store_count, capacity, requests,
    shard_ref, tile_ref, dec_ref, qw_hbm, kvw_hbm, ow_hbm, tiles_hbm, out_ref,
    rows, neigh, table, tiles, outgoing, arrived, qw, kvw, ow, q_buf, k_buf, v_buf, att, part, xrecv, up, down,
    load_sem, a2a_send, a2a_recv, rows_send, rows_recv, neigh_send, neigh_recv,
    part_send, part_recv, chain_send, up_recv, down_recv,
):
    store = lax.axis_index("store")
    tensor = lax.axis_index("tensor")
    z = lax.div(tensor, 2)
    x = lax.rem(tensor, 2)
    top = LINE - 1
    partner = z * 2 + 1 - x
    q_factor = 1.0 / math.sqrt(HD)
    head_count = qw.shape[1] // HD
    tile_rows = arrived.shape[1]

    loads = [
        pltpu.make_async_copy(src, dst, load_sem.at[i])
        for i, (src, dst) in enumerate(
            ((tiles_hbm, tiles), (kvw_hbm, kvw), (qw_hbm, qw), (ow_hbm, ow))
        )
    ]
    own_slots = pl.ds(store * capacity, capacity)
    for load in loads:
        load.start()

    barrier = pltpu.get_barrier_semaphore()
    for k in range(1, store_count):
        peer = lax.rem(store + k, store_count)
        pl.semaphore_signal(barrier, inc=1, device_id=(peer, tensor), device_id_type=MESH)
    pl.semaphore_signal(barrier, inc=1, device_id=(store, partner), device_id_type=MESH)

    @pl.when(z > 0)
    def _():
        pl.semaphore_signal(barrier, inc=1, device_id=(store, tensor - 2), device_id_type=MESH)

    @pl.when(z < top)
    def _():
        pl.semaphore_signal(barrier, inc=1, device_id=(store, tensor + 2), device_id_type=MESH)

    @pl.loop(0, dec_ref.shape[0] // 16)
    def _(i):
        at = pl.ds(pl.multiple_of(i * 16, 16), 16)
        wide = dec_ref[at, :].astype(F32)
        scale = lax.rsqrt(jnp.mean(wide * wide, axis=1, keepdims=True) + 1e-05)
        rows[tensor, at, :] = (wide * scale).astype(BF16)

    inner = (z > 0) & (z < top)

    @pl.when(inner)
    def _():
        pl.semaphore_wait(barrier, store_count + 2)

    @pl.when(jnp.logical_not(inner))
    def _():
        pl.semaphore_wait(barrier, store_count + 1)

    def tiles_copy(k):
        peer = lax.rem(store + k, store_count)
        return pltpu.make_async_remote_copy(
            src_ref=outgoing.at[pl.ds(peer * capacity, capacity)],
            dst_ref=arrived.at[own_slots],
            send_sem=a2a_send.at[k - 1],
            recv_sem=a2a_recv.at[k - 1],
            device_id=(peer, tensor),
            device_id_type=MESH,
        )

    def block_copy(buf, send, recv, way, j):
        target = (tensor + 2, tensor - 2, partner)[way]
        return pltpu.make_async_remote_copy(
            src_ref=buf.at[j],
            dst_ref=buf.at[j],
            send_sem=send.at[way, j],
            recv_sem=recv.at[j],
            device_id=(store, target),
            device_id_type=MESH,
        )

    row_copy = functools.partial(block_copy, rows, rows_send, rows_recv)
    neigh_copy = functools.partial(block_copy, neigh, neigh_send, neigh_recv)

    def send_own(copy):
        @pl.when(z < top)
        def _():
            copy(0, tensor).start()

        @pl.when(z > 0)
        def _():
            copy(1, tensor).start()

        copy(2, tensor).start()

    def forward(copy, d):
        @pl.when(z - d >= 0)
        def _():
            j = tensor - 2 * d
            copy(0, j).wait_recv()

            @pl.when(z < top)
            def _():
                copy(0, j).start()

            copy(2, j).start()

        @pl.when(z + d <= top)
        def _():
            j = tensor + 2 * d
            copy(1, j).wait_recv()

            @pl.when(z > 0)
            def _():
                copy(1, j).start()

            copy(2, j).start()

    send_own(row_copy)

    for s in range(store_count):
        wanted = [jnp.int32(0)] * capacity
        seen = jnp.int32(0)
        for r in range(requests):
            n, b = r % NEIGH, (s * requests + r) // NEIGH
            hit = shard_ref[n, b] == store
            tile = tile_ref[n, b]
            for c in range(min(r + 1, capacity)):
                wanted[c] = jnp.where(hit & (seen == c), tile, wanted[c])
            seen = seen + hit.astype(jnp.int32)
        for c in range(capacity):
            table[s * capacity + c] = wanted[c]

    loads[0].wait()

    @pl.loop(0, store_count * capacity)
    def _(i):
        outgoing[i] = tiles[table[i]]

    for k in range(1, store_count):
        tiles_copy(k).start()

    for c in range(capacity):
        arrived[store * capacity + c] = outgoing[store * capacity + c]
    for k in range(1, store_count):
        tiles_copy(k).wait_recv()

    counts = [jnp.int32(0)] * store_count
    for r in range(requests):
        shard = shard_ref[r % NEIGH, store * (requests // NEIGH) + r // NEIGH]
        slot = shard * capacity
        for k in range(store_count):
            slot = slot + jnp.where(shard == k, counts[k], 0)
            counts[k] = counts[k] + (shard == k).astype(jnp.int32)
        neigh[tensor, pl.ds(r * tile_rows, tile_rows), :] = arrived[slot]

    send_own(neigh_copy)

    def project(j):
        source = neigh[j]
        for a, dst in ((0, k_buf), (1, v_buf)):
            got = jnp.dot(source, kvw[a], preferred_element_type=F32).astype(BF16)
            dst[j] = got.reshape(dst.shape[1:])

    loads[1].wait()
    project(tensor)

    @pl.loop(1, LINE)
    def _(d):
        forward(row_copy, d)
        forward(neigh_copy, d)

        @pl.when(z - d >= 0)
        def _():
            project(tensor - 2 * d)

        @pl.when(z + d <= top)
        def _():
            project(tensor + 2 * d)

    for p in range(LINE):
        row_copy(2, p * 2 + 1 - x).wait_recv()
    loads[2].wait()

    @pl.loop(0, qw.shape[1] // 256)
    def _(c):
        at = pl.ds(pl.multiple_of(c * 256, 256), 256)
        all_rows = rows[...].reshape(-1, rows.shape[2])
        got = jnp.dot(all_rows, qw[:, at], preferred_element_type=F32)
        q_buf[:, :, at] = (got * q_factor).astype(BF16).reshape(q_buf.shape[0], BLOCK, 256)

    half = lax.div(z, 2)
    near = z + half * (3 - 2 * z)

    def place(k):
        o = (3, 2 - 2 * near, 1 + near, near)[k]
        return o + half * (3 - 2 * o)

    for k in reversed(range(LINE)):
        j = place(k) * 2 + 1 - x
        neigh_copy(2, j).wait_recv()
        project(j)
    loads[3].wait()

    def part_copy(p):
        return pltpu.make_async_remote_copy(
            src_ref=part.at[p, 1 - x],
            dst_ref=xrecv.at[p],
            send_sem=part_send.at[p],
            recv_sem=part_recv.at[p],
            device_id=(store, partner),
            device_id_type=MESH,
        )

    def chain_copy(way, p):
        return pltpu.make_async_remote_copy(
            src_ref=part.at[p, x],
            dst_ref=(up, down)[way].at[p],
            send_sem=chain_send.at[p],
            recv_sem=(up_recv, down_recv)[way].at[p],
            device_id=(store, (tensor + 2, tensor - 2)[way]),
            device_id_type=MESH,
        )

    def attend(p):
        @pl.loop(0, 2)
        def _(i):
            b = p * 2 + i
            for h in range(head_count):
                cols = slice(h * HD, (h + 1) * HD)
                keys = k_buf[:, b, :, cols].reshape(-1, HD)
                values = v_buf[:, b, :, cols].reshape(-1, HD)
                scores = lax.dot_general(
                    q_buf[b, :, cols], keys, (((1,), (1,)), ((), ())),
                    preferred_element_type=F32,
                )
                expo = jnp.exp(scores)
                weights = (expo / jnp.sum(expo, axis=1, keepdims=True)).astype(BF16)
                got = jnp.dot(weights, values, preferred_element_type=F32)
                att[i, :, cols] = got.astype(BF16)

        @pl.loop(0, ow.shape[1] // 512)
        def _(c):
            at = pl.ds(pl.multiple_of(c * 512, 512), 512)
            both = att[...].reshape(-1, att.shape[2])
            got = jnp.dot(both, ow[:, at], preferred_element_type=F32).astype(BF16)
            part[p, :, :, at] = got.reshape(2, BLOCK, 512)

        part_copy(p).start()

    def add(p, *terms):
        @pl.loop(0, BLOCK // 16)
        def _(i):
            at = pl.ds(pl.multiple_of(i * 16, 16), 16)
            total = part[p, x, at, :].astype(F32)
            for term in terms:
                total = total + term[p, at, :].astype(F32)
            part[p, x, at, :] = total.astype(BF16)

    def pass_on(p):
        part_copy(p).wait_recv()
        add(p, xrecv)

        @pl.when(p > z)
        def _():
            @pl.when(z > 0)
            def _():
                chain_copy(0, p).wait_recv()
                add(p, up)

            chain_copy(0, p).start()

        @pl.when(p < z)
        def _():
            @pl.when(z < top)
            def _():
                chain_copy(1, p).wait_recv()
                add(p, down)

            chain_copy(1, p).start()

    attend(place(0))
    attend(place(1))
    pass_on(place(0))
    attend(place(2))
    pass_on(place(1))
    attend(place(3))
    pass_on(place(2))
    part_copy(z).wait_recv()
    add(z, xrecv)

    @pl.when(z > 0)
    def _():
        chain_copy(0, z).wait_recv()
        add(z, up)

    @pl.when(z < top)
    def _():
        chain_copy(1, z).wait_recv()
        add(z, down)

    out_ref[...] = part[z, x]

    for k in range(1, store_count):
        tiles_copy(k).wait_send()
    for copy in (row_copy, neigh_copy):
        for p in range(LINE):
            j = p * 2 + x

            @pl.when((p <= z) & (z < top))
            def _():
                copy(0, j).wait_send()

            @pl.when((p >= z) & (z > 0))
            def _():
                copy(1, j).wait_send()

            copy(2, j).wait_send()
    for p in range(LINE):
        part_copy(p).wait_send()

        @pl.when(z != p)
        def _():
            chain_copy(0, p).wait_send()


def kernel_body(
    decoder_rows, q_weight, kv_weight, out_weight, store_tiles, neighbour_shard, neighbour_tile
):
    tensor_count = lax.axis_size("tensor")
    store_count = lax.axis_size("store")
    local_rows, width = decoder_rows.shape
    blocks = tensor_count * local_rows // BLOCK
    requests = blocks * NEIGH
    capacity = 3 * requests // (2 * store_count)
    slots = store_count * capacity
    tile_rows, enc = store_tiles.shape[1:]
    head_cols = q_weight.shape[1]
    hbm = pl.BlockSpec(memory_space=pl.ANY)
    smem = pl.BlockSpec(memory_space=pltpu.SMEM)
    vmem = pl.BlockSpec(memory_space=pltpu.VMEM)
    dma = pltpu.SemaphoreType.DMA
    block_keys = NEIGH * tile_rows
    return pl.pallas_call(
        functools.partial(main_kernel, store_count, capacity, requests),
        out_shape=jax.ShapeDtypeStruct((local_rows, width), BF16),
        in_specs=[smem, smem, vmem, hbm, hbm, hbm, hbm],
        out_specs=vmem,
        scratch_shapes=[
            pltpu.VMEM((tensor_count, local_rows, width), BF16),
            pltpu.VMEM((tensor_count, requests * tile_rows, enc), BF16),
            pltpu.SMEM((slots,), jnp.int32),
            pltpu.VMEM(store_tiles.shape, BF16),
            pltpu.VMEM((slots, tile_rows, enc), BF16),
            pltpu.VMEM((slots, tile_rows, enc), BF16),
            pltpu.VMEM(q_weight.shape, BF16),
            pltpu.VMEM(kv_weight.shape, BF16),
            pltpu.VMEM(out_weight.shape, BF16),
            pltpu.VMEM((blocks, BLOCK, head_cols), BF16),
            pltpu.VMEM((tensor_count, blocks, block_keys, head_cols), BF16),
            pltpu.VMEM((tensor_count, blocks, block_keys, head_cols), BF16),
            pltpu.VMEM((2, BLOCK, head_cols), BF16),
            pltpu.VMEM((LINE, 2, BLOCK, width), BF16),
            pltpu.VMEM((LINE, BLOCK, width), BF16),
            pltpu.VMEM((LINE, BLOCK, width), BF16),
            pltpu.VMEM((LINE, BLOCK, width), BF16),
            dma((4,)),
            dma((store_count - 1,)),
            dma((store_count - 1,)),
            dma((3, tensor_count)),
            dma((tensor_count,)),
            dma((3, tensor_count)),
            dma((tensor_count,)),
            dma((LINE,)),
            dma((LINE,)),
            dma((LINE,)),
            dma((LINE,)),
            dma((LINE,)),
        ],
        compiler_params=pltpu.CompilerParams(
            collective_id=0, has_side_effects=True, vmem_limit_bytes=56 * 2**20
        ),
    )(
        neighbour_shard.T, neighbour_tile.T, decoder_rows, q_weight, kv_weight, out_weight,
        store_tiles,
    )


def plain_body(
    decoder_rows, q_weight, kv_weight, out_weight, store_tiles, neighbour_shard, neighbour_tile
):
    tensor_count = lax.axis_size("tensor")
    store_count = lax.axis_size("store")
    my_sequence = lax.axis_index("store")
    local_rows = decoder_rows.shape[0]
    seq_len = local_rows * tensor_count
    block_count = seq_len // BLOCK
    request_count = block_count * NEIGH
    capacity = 3 * request_count // (2 * store_count)
    head_cols = q_weight.shape[1]
    head_count = head_cols // HD
    q_factor = 1.0 / math.sqrt(HD)
    rows_wide = decoder_rows.astype(jnp.float32)
    normed = (
        rows_wide * lax.rsqrt(jnp.mean(rows_wide * rows_wide, axis=1, keepdims=True) + 1e-05)
    ).astype(jnp.bfloat16)
    queries = (
        jnp.dot(
            lax.all_gather(normed, "tensor", axis=0, tiled=True),
            q_weight,
            preferred_element_type=jnp.float32,
        )
        * q_factor
    ).astype(jnp.bfloat16)
    shard_table = neighbour_shard.reshape(store_count, request_count)
    tile_table = neighbour_tile.reshape(store_count, request_count)
    positions = jnp.arange(request_count, dtype=jnp.int32)
    before_mask = positions[None, :] < positions[:, None]
    same_shard = shard_table[:, :, None] == shard_table[:, None, :]
    rank_table = jnp.sum((same_shard & before_mask[None]).astype(jnp.int32), axis=2)
    served_here = shard_table == my_sequence
    slot_ids = jnp.arange(capacity, dtype=jnp.int32)
    slot_match = (
        served_here[:, :, None] & (rank_table[:, :, None] == slot_ids[None, None, :])
    ).astype(jnp.int32)
    slot_tile = jnp.sum(slot_match * tile_table[:, :, None], axis=1)
    outgoing = jnp.take(store_tiles, slot_tile.reshape(-1), axis=0)
    arrived = lax.all_to_all(outgoing, "store", split_axis=0, concat_axis=0, tiled=True)
    own_shard = lax.dynamic_index_in_dim(shard_table, my_sequence, 0, keepdims=False)
    own_rank = lax.dynamic_index_in_dim(rank_table, my_sequence, 0, keepdims=False)
    slot_index = own_shard * capacity + own_rank
    picked = jnp.take(arrived, slot_index, axis=0)
    projected = jnp.einsum(
        "rne,ced->rncd",
        lax.all_gather(picked, "tensor", axis=1, tiled=True),
        kv_weight,
        preferred_element_type=jnp.float32,
    )
    keys_values = projected.astype(jnp.bfloat16)
    keyed = keys_values.reshape(block_count, NEIGH * NTOK, 2, head_count, HD)
    query_blocks = queries.reshape(block_count, BLOCK, head_count, HD)
    scores = jnp.einsum(
        "cqhd,ckhd->chqk", query_blocks, keyed[:, :, 0], preferred_element_type=jnp.float32
    )
    expo_scores = jnp.exp(scores)
    weights = (expo_scores / jnp.sum(expo_scores, axis=3, keepdims=True)).astype(jnp.bfloat16)
    attended = jnp.einsum(
        "chqk,ckhd->cqhd", weights, keyed[:, :, 1], preferred_element_type=jnp.float32
    )
    attended = attended.astype(jnp.bfloat16).reshape(seq_len, head_cols)
    return lax.psum_scatter(
        jnp.dot(attended, out_weight, preferred_element_type=jnp.float32).astype(jnp.bfloat16),
        "tensor",
        scatter_dimension=0,
        tiled=True,
    )


def body(*args):
    fits = (
        lax.axis_size("tensor") == 2 * LINE
        and args[0].shape[0] == BLOCK
        and args[4].shape[1] % 16 == 0
    )
    return (kernel_body if fits else plain_body)(*args)


def solution(mesh):
    in_specs = (
        P(("store", "tensor"), None),
        P(None, "tensor"),
        P(None, None, "tensor"),
        P("tensor", None),
        P("store", "tensor", None),
        P(),
        P(),
    )
    out_specs = P(("store", "tensor"), None)
    return jax.shard_map(body, mesh=mesh, in_specs=in_specs, out_specs=out_specs, check_vma=False)
```

```python
import functools
import math

import jax
import jax.numpy as jnp
from jax import lax
from jax.experimental import pallas as pl
from jax.experimental.pallas import tpu as pltpu
from jax.sharding import PartitionSpec as P

HD = 128
BLOCK = 64
NTOK = 128
NEIGH = 2
LINE = 4
F32 = jnp.float32
BF16 = jnp.bfloat16
MESH = pl.DeviceIdType.MESH


def main_kernel(
    store_count, capacity, requests,
    shard_ref, tile_ref, dec_ref, qw_hbm, kvw_hbm, ow_hbm, tiles_hbm, out_ref,
    rows, neigh, table, tiles, outgoing, arrived, qw, kvw, ow, q_buf, k_buf, v_buf, att,
    part, xrecv, up, down, side_up, side_down, side_x,
    load_sem, a2a_send, a2a_recv, rows_send, rows_recv, neigh_send, neigh_recv,
    part_send, part_recv, chain_send, up_recv, down_recv,
    edge_send, edge_recv, edge_x, side_send, side_up_recv, side_down_recv, side_x_sem,
):
    store = lax.axis_index("store")
    tensor = lax.axis_index("tensor")
    z = lax.div(tensor, 2)
    x = lax.rem(tensor, 2)
    top = LINE - 1
    partner = z * 2 + 1 - x
    q_factor = 1.0 / math.sqrt(HD)
    head_count = qw.shape[1] // HD
    tile_rows = arrived.shape[1]
    width = rows.shape[2]
    cut = width * 11 // 16
    side = width * 13 // 16

    loads = [
        pltpu.make_async_copy(src, dst, load_sem.at[i])
        for i, (src, dst) in enumerate(
            ((tiles_hbm, tiles), (kvw_hbm, kvw), (qw_hbm, qw), (ow_hbm, ow))
        )
    ]
    own_slots = pl.ds(store * capacity, capacity)
    for load in loads:
        load.start()

    barrier = pltpu.get_barrier_semaphore()
    for k in range(1, store_count):
        peer = lax.rem(store + k, store_count)
        pl.semaphore_signal(barrier, inc=1, device_id=(peer, tensor), device_id_type=MESH)
    pl.semaphore_signal(barrier, inc=1, device_id=(store, partner), device_id_type=MESH)

    @pl.when(z > 0)
    def _():
        pl.semaphore_signal(barrier, inc=1, device_id=(store, tensor - 2), device_id_type=MESH)

    @pl.when(z < top)
    def _():
        pl.semaphore_signal(barrier, inc=1, device_id=(store, tensor + 2), device_id_type=MESH)

    @pl.loop(0, dec_ref.shape[0] // 16)
    def _(i):
        at = pl.ds(pl.multiple_of(i * 16, 16), 16)
        wide = dec_ref[at, :].astype(F32)
        scale = lax.rsqrt(jnp.mean(wide * wide, axis=1, keepdims=True) + 1e-05)
        rows[tensor, at, :] = (wide * scale).astype(BF16)

    inner = (z > 0) & (z < top)

    @pl.when(inner)
    def _():
        pl.semaphore_wait(barrier, store_count + 2)

    @pl.when(jnp.logical_not(inner))
    def _():
        pl.semaphore_wait(barrier, store_count + 1)

    def tiles_copy(k):
        peer = lax.rem(store + k, store_count)
        return pltpu.make_async_remote_copy(
            src_ref=outgoing.at[pl.ds(peer * capacity, capacity)],
            dst_ref=arrived.at[own_slots],
            send_sem=a2a_send.at[k - 1],
            recv_sem=a2a_recv.at[k - 1],
            device_id=(peer, tensor),
            device_id_type=MESH,
        )

    def block_copy(buf, columns, send, recv, way, j):
        target = (tensor + 2, tensor - 2, partner)[way]
        return pltpu.make_async_remote_copy(
            src_ref=buf.at[j, :, pl.ds(0, columns)],
            dst_ref=buf.at[j, :, pl.ds(0, columns)],
            send_sem=send.at[way, j],
            recv_sem=recv.at[j],
            device_id=(store, target),
            device_id_type=MESH,
        )

    row_copy = functools.partial(block_copy, rows, cut, rows_send, rows_recv)
    neigh_copy = functools.partial(block_copy, neigh, neigh.shape[2], neigh_send, neigh_recv)

    def edge_across(j):
        at = rows.at[j, :, pl.ds(cut, width - cut)]
        return pltpu.make_async_remote_copy(
            src_ref=at,
            dst_ref=at,
            send_sem=edge_x.at[0],
            recv_sem=edge_x.at[1],
            device_id=(store, partner),
            device_id_type=MESH,
        )

    def edge_copy(way, p):
        at = rows.at[pl.ds(p * 2, 2), :, pl.ds(cut, width - cut)]
        return pltpu.make_async_remote_copy(
            src_ref=at,
            dst_ref=at,
            send_sem=edge_send.at[way, p],
            recv_sem=edge_recv.at[p],
            device_id=(store, (tensor + 2, tensor - 2)[way]),
            device_id_type=MESH,
        )

    def send_own(copy):
        @pl.when(z < top)
        def _():
            copy(0, tensor).start()

        @pl.when(z > 0)
        def _():
            copy(1, tensor).start()

        copy(2, tensor).start()

    def forward(copy, d):
        @pl.when(z - d >= 0)
        def _():
            j = tensor - 2 * d
            copy(0, j).wait_recv()

            @pl.when(z < top)
            def _():
                copy(0, j).start()

            copy(2, j).start()

        @pl.when(z + d <= top)
        def _():
            j = tensor + 2 * d
            copy(1, j).wait_recv()

            @pl.when(z > 0)
            def _():
                copy(1, j).start()

            copy(2, j).start()

    edge_across(tensor).start()
    send_own(row_copy)

    for s in range(store_count):
        wanted = [jnp.int32(0)] * capacity
        seen = jnp.int32(0)
        for r in range(requests):
            n, b = r % NEIGH, (s * requests + r) // NEIGH
            hit = shard_ref[n, b] == store
            tile = tile_ref[n, b]
            for c in range(min(r + 1, capacity)):
                wanted[c] = jnp.where(hit & (seen == c), tile, wanted[c])
            seen = seen + hit.astype(jnp.int32)
        for c in range(capacity):
            table[s * capacity + c] = wanted[c]

    loads[0].wait()

    @pl.loop(0, store_count * capacity)
    def _(i):
        outgoing[i] = tiles[table[i]]

    for k in range(1, store_count):
        tiles_copy(k).start()

    for c in range(capacity):
        arrived[store * capacity + c] = outgoing[store * capacity + c]
    for k in range(1, store_count):
        tiles_copy(k).wait_recv()

    counts = [jnp.int32(0)] * store_count
    for r in range(requests):
        shard = shard_ref[r % NEIGH, store * (requests // NEIGH) + r // NEIGH]
        slot = shard * capacity
        for k in range(store_count):
            slot = slot + jnp.where(shard == k, counts[k], 0)
            counts[k] = counts[k] + (shard == k).astype(jnp.int32)
        neigh[tensor, pl.ds(r * tile_rows, tile_rows), :] = arrived[slot]

    send_own(neigh_copy)
    edge_across(partner).wait_recv()

    @pl.when(z < top)
    def _():
        edge_copy(0, z).start()

    @pl.when(z > 0)
    def _():
        edge_copy(1, z).start()

    def project(j):
        source = neigh[j]
        for a, dst in ((0, k_buf), (1, v_buf)):
            got = jnp.dot(source, kvw[a], preferred_element_type=F32).astype(BF16)
            dst[j] = got.reshape(dst.shape[1:])

    loads[1].wait()
    project(tensor)

    @pl.loop(1, LINE)
    def _(d):
        forward(row_copy, d)

        @pl.when(z - d >= 0)
        def _():
            edge_copy(0, z - d).wait_recv()

            @pl.when(z < top)
            def _():
                edge_copy(0, z - d).start()

        @pl.when(z + d <= top)
        def _():
            edge_copy(1, z + d).wait_recv()

            @pl.when(z > 0)
            def _():
                edge_copy(1, z + d).start()

        forward(neigh_copy, d)

        @pl.when(z - d >= 0)
        def _():
            project(tensor - 2 * d)

        @pl.when(z + d <= top)
        def _():
            project(tensor + 2 * d)

    for p in range(LINE):
        row_copy(2, p * 2 + 1 - x).wait_recv()
    loads[2].wait()

    @pl.loop(0, qw.shape[1] // 256)
    def _(c):
        at = pl.ds(pl.multiple_of(c * 256, 256), 256)
        all_rows = rows[...].reshape(-1, rows.shape[2])
        got = jnp.dot(all_rows, qw[:, at], preferred_element_type=F32)
        q_buf[:, :, at] = (got * q_factor).astype(BF16).reshape(q_buf.shape[0], BLOCK, 256)

    half = lax.div(z, 2)
    near = z + half * (3 - 2 * z)

    def place(k):
        o = (3, 2 - 2 * near, 1 + near, near)[k]
        return o + half * (3 - 2 * o)

    for k in reversed(range(LINE)):
        j = place(k) * 2 + 1 - x
        neigh_copy(2, j).wait_recv()
        project(j)
    loads[3].wait()

    def part_copy(p):
        return pltpu.make_async_remote_copy(
            src_ref=part.at[p, 1 - x, :, pl.ds(0, side)],
            dst_ref=xrecv.at[p],
            send_sem=part_send.at[p],
            recv_sem=part_recv.at[p],
            device_id=(store, partner),
            device_id_type=MESH,
        )

    def chain_copy(way, p):
        return pltpu.make_async_remote_copy(
            src_ref=part.at[p, x, :, pl.ds(0, side)],
            dst_ref=(up, down)[way].at[p],
            send_sem=chain_send.at[p],
            recv_sem=(up_recv, down_recv)[way].at[p],
            device_id=(store, (tensor + 2, tensor - 2)[way]),
            device_id_type=MESH,
        )

    def side_copy(way, p):
        return pltpu.make_async_remote_copy(
            src_ref=part.at[p, :, :, pl.ds(side, width - side)],
            dst_ref=(side_up, side_down)[way].at[p],
            send_sem=side_send.at[p],
            recv_sem=(side_up_recv, side_down_recv)[way].at[p],
            device_id=(store, (tensor + 2, tensor - 2)[way]),
            device_id_type=MESH,
        )

    def side_across():
        return pltpu.make_async_remote_copy(
            src_ref=part.at[z, 1 - x, :, pl.ds(side, width - side)],
            dst_ref=side_x,
            send_sem=side_x_sem.at[0],
            recv_sem=side_x_sem.at[1],
            device_id=(store, partner),
            device_id_type=MESH,
        )

    def add_side(p, term):
        @pl.loop(0, 2 * BLOCK // 16)
        def _(i):
            c = lax.div(i, BLOCK // 16)
            at = pl.ds(pl.multiple_of(lax.rem(i, BLOCK // 16) * 16, 16), 16)
            total = part[p, c, at, side:].astype(F32) + term[p, c, at, :].astype(F32)
            part[p, c, at, side:] = total.astype(BF16)

    def pass_side(p):
        @pl.when(p > z)
        def _():
            @pl.when(z > 0)
            def _():
                side_copy(0, p).wait_recv()
                add_side(p, side_up)

            side_copy(0, p).start()

        @pl.when(p < z)
        def _():
            @pl.when(z < top)
            def _():
                side_copy(1, p).wait_recv()
                add_side(p, side_down)

            side_copy(1, p).start()

    def attend(p):
        @pl.loop(0, 2)
        def _(i):
            b = p * 2 + i
            for h in range(head_count):
                cols = slice(h * HD, (h + 1) * HD)
                keys = k_buf[:, b, :, cols].reshape(-1, HD)
                values = v_buf[:, b, :, cols].reshape(-1, HD)
                scores = lax.dot_general(
                    q_buf[b, :, cols], keys, (((1,), (1,)), ((), ())),
                    preferred_element_type=F32,
                )
                expo = jnp.exp(scores)
                weights = (expo / jnp.sum(expo, axis=1, keepdims=True)).astype(BF16)
                got = jnp.dot(weights, values, preferred_element_type=F32)
                att[i, :, cols] = got.astype(BF16)

        @pl.loop(0, ow.shape[1] // 512)
        def _(c):
            at = pl.ds(pl.multiple_of(c * 512, 512), 512)
            both = att[...].reshape(-1, att.shape[2])
            got = jnp.dot(both, ow[:, at], preferred_element_type=F32).astype(BF16)
            part[p, :, :, at] = got.reshape(2, BLOCK, 512)

        part_copy(p).start()

    def add(p, *terms):
        @pl.loop(0, BLOCK // 16)
        def _(i):
            at = pl.ds(pl.multiple_of(i * 16, 16), 16)
            total = part[p, x, at, :side].astype(F32)
            for term in terms:
                total = total + term[p, at, :].astype(F32)
            part[p, x, at, :side] = total.astype(BF16)

    def pass_on(p):
        part_copy(p).wait_recv()
        add(p, xrecv)

        @pl.when(p > z)
        def _():
            @pl.when(z > 0)
            def _():
                chain_copy(0, p).wait_recv()
                add(p, up)

            chain_copy(0, p).start()

        @pl.when(p < z)
        def _():
            @pl.when(z < top)
            def _():
                chain_copy(1, p).wait_recv()
                add(p, down)

            chain_copy(1, p).start()

    attend(place(0))
    attend(place(1))
    pass_side(place(0))
    pass_on(place(0))
    attend(place(2))
    pass_side(place(1))
    pass_on(place(1))
    attend(place(3))
    pass_side(place(2))
    pass_on(place(2))
    @pl.when(z > 0)
    def _():
        side_copy(0, z).wait_recv()
        add_side(z, side_up)

    @pl.when(z < top)
    def _():
        side_copy(1, z).wait_recv()
        add_side(z, side_down)

    side_across().start()
    part_copy(z).wait_recv()
    add(z, xrecv)

    @pl.when(z > 0)
    def _():
        chain_copy(0, z).wait_recv()
        add(z, up)

    @pl.when(z < top)
    def _():
        chain_copy(1, z).wait_recv()
        add(z, down)

    out_ref[:, :side] = part[z, x, :, :side]
    side_across().wait_recv()
    last = part[z, x, :, side:].astype(F32) + side_x[...].astype(F32)
    out_ref[:, side:] = last.astype(BF16)
    side_across().wait_send()
    edge_across(tensor).wait_send()

    for k in range(1, store_count):
        tiles_copy(k).wait_send()
    for copy in (row_copy, neigh_copy):
        for p in range(LINE):
            j = p * 2 + x

            @pl.when((p <= z) & (z < top))
            def _():
                copy(0, j).wait_send()

            @pl.when((p >= z) & (z > 0))
            def _():
                copy(1, j).wait_send()

            copy(2, j).wait_send()
    for p in range(LINE):
        part_copy(p).wait_send()

        @pl.when(z != p)
        def _():
            chain_copy(0, p).wait_send()
            side_copy(0, p).wait_send()

        @pl.when((p <= z) & (z < top))
        def _():
            edge_copy(0, p).wait_send()

        @pl.when((p >= z) & (z > 0))
        def _():
            edge_copy(1, p).wait_send()


def kernel_body(
    decoder_rows, q_weight, kv_weight, out_weight, store_tiles, neighbour_shard, neighbour_tile
):
    tensor_count = lax.axis_size("tensor")
    store_count = lax.axis_size("store")
    local_rows, width = decoder_rows.shape
    blocks = tensor_count * local_rows // BLOCK
    requests = blocks * NEIGH
    capacity = 3 * requests // (2 * store_count)
    slots = store_count * capacity
    tile_rows, enc = store_tiles.shape[1:]
    head_cols = q_weight.shape[1]
    hbm = pl.BlockSpec(memory_space=pl.ANY)
    smem = pl.BlockSpec(memory_space=pltpu.SMEM)
    vmem = pl.BlockSpec(memory_space=pltpu.VMEM)
    dma = pltpu.SemaphoreType.DMA
    block_keys = NEIGH * tile_rows
    side = width * 13 // 16
    return pl.pallas_call(
        functools.partial(main_kernel, store_count, capacity, requests),
        out_shape=jax.ShapeDtypeStruct((local_rows, width), BF16),
        in_specs=[smem, smem, vmem, hbm, hbm, hbm, hbm],
        out_specs=vmem,
        scratch_shapes=[
            pltpu.VMEM((tensor_count, local_rows, width), BF16),
            pltpu.VMEM((tensor_count, requests * tile_rows, enc), BF16),
            pltpu.SMEM((slots,), jnp.int32),
            pltpu.VMEM(store_tiles.shape, BF16),
            pltpu.VMEM((slots, tile_rows, enc), BF16),
            pltpu.VMEM((slots, tile_rows, enc), BF16),
            pltpu.VMEM(q_weight.shape, BF16),
            pltpu.VMEM(kv_weight.shape, BF16),
            pltpu.VMEM(out_weight.shape, BF16),
            pltpu.VMEM((blocks, BLOCK, head_cols), BF16),
            pltpu.VMEM((tensor_count, blocks, block_keys, head_cols), BF16),
            pltpu.VMEM((tensor_count, blocks, block_keys, head_cols), BF16),
            pltpu.VMEM((2, BLOCK, head_cols), BF16),
            pltpu.VMEM((LINE, 2, BLOCK, width), BF16),
            pltpu.VMEM((LINE, BLOCK, side), BF16),
            pltpu.VMEM((LINE, BLOCK, side), BF16),
            pltpu.VMEM((LINE, BLOCK, side), BF16),
            pltpu.VMEM((LINE, 2, BLOCK, width - side), BF16),
            pltpu.VMEM((LINE, 2, BLOCK, width - side), BF16),
            pltpu.VMEM((BLOCK, width - side), BF16),
            dma((4,)),
            dma((store_count - 1,)),
            dma((store_count - 1,)),
            dma((3, tensor_count)),
            dma((tensor_count,)),
            dma((3, tensor_count)),
            dma((tensor_count,)),
            dma((LINE,)),
            dma((LINE,)),
            dma((LINE,)),
            dma((LINE,)),
            dma((LINE,)),
            dma((2, LINE)),
            dma((LINE,)),
            dma((2,)),
            dma((LINE,)),
            dma((LINE,)),
            dma((LINE,)),
            dma((2,)),
        ],
        compiler_params=pltpu.CompilerParams(
            collective_id=0, has_side_effects=True, vmem_limit_bytes=56 * 2**20
        ),
    )(
        neighbour_shard.T, neighbour_tile.T, decoder_rows, q_weight, kv_weight, out_weight,
        store_tiles,
    )


def plain_body(
    decoder_rows, q_weight, kv_weight, out_weight, store_tiles, neighbour_shard, neighbour_tile
):
    tensor_count = lax.axis_size("tensor")
    store_count = lax.axis_size("store")
    my_sequence = lax.axis_index("store")
    local_rows = decoder_rows.shape[0]
    seq_len = local_rows * tensor_count
    block_count = seq_len // BLOCK
    request_count = block_count * NEIGH
    capacity = 3 * request_count // (2 * store_count)
    head_cols = q_weight.shape[1]
    head_count = head_cols // HD
    q_factor = 1.0 / math.sqrt(HD)
    rows_wide = decoder_rows.astype(jnp.float32)
    normed = (
        rows_wide * lax.rsqrt(jnp.mean(rows_wide * rows_wide, axis=1, keepdims=True) + 1e-05)
    ).astype(jnp.bfloat16)
    queries = (
        jnp.dot(
            lax.all_gather(normed, "tensor", axis=0, tiled=True),
            q_weight,
            preferred_element_type=jnp.float32,
        )
        * q_factor
    ).astype(jnp.bfloat16)
    shard_table = neighbour_shard.reshape(store_count, request_count)
    tile_table = neighbour_tile.reshape(store_count, request_count)
    positions = jnp.arange(request_count, dtype=jnp.int32)
    before_mask = positions[None, :] < positions[:, None]
    same_shard = shard_table[:, :, None] == shard_table[:, None, :]
    rank_table = jnp.sum((same_shard & before_mask[None]).astype(jnp.int32), axis=2)
    served_here = shard_table == my_sequence
    slot_ids = jnp.arange(capacity, dtype=jnp.int32)
    slot_match = (
        served_here[:, :, None] & (rank_table[:, :, None] == slot_ids[None, None, :])
    ).astype(jnp.int32)
    slot_tile = jnp.sum(slot_match * tile_table[:, :, None], axis=1)
    outgoing = jnp.take(store_tiles, slot_tile.reshape(-1), axis=0)
    arrived = lax.all_to_all(outgoing, "store", split_axis=0, concat_axis=0, tiled=True)
    own_shard = lax.dynamic_index_in_dim(shard_table, my_sequence, 0, keepdims=False)
    own_rank = lax.dynamic_index_in_dim(rank_table, my_sequence, 0, keepdims=False)
    slot_index = own_shard * capacity + own_rank
    picked = jnp.take(arrived, slot_index, axis=0)
    projected = jnp.einsum(
        "rne,ced->rncd",
        lax.all_gather(picked, "tensor", axis=1, tiled=True),
        kv_weight,
        preferred_element_type=jnp.float32,
    )
    keys_values = projected.astype(jnp.bfloat16)
    keyed = keys_values.reshape(block_count, NEIGH * NTOK, 2, head_count, HD)
    query_blocks = queries.reshape(block_count, BLOCK, head_count, HD)
    scores = jnp.einsum(
        "cqhd,ckhd->chqk", query_blocks, keyed[:, :, 0], preferred_element_type=jnp.float32
    )
    expo_scores = jnp.exp(scores)
    weights = (expo_scores / jnp.sum(expo_scores, axis=3, keepdims=True)).astype(jnp.bfloat16)
    attended = jnp.einsum(
        "chqk,ckhd->cqhd", weights, keyed[:, :, 1], preferred_element_type=jnp.float32
    )
    attended = attended.astype(jnp.bfloat16).reshape(seq_len, head_cols)
    return lax.psum_scatter(
        jnp.dot(attended, out_weight, preferred_element_type=jnp.float32).astype(jnp.bfloat16),
        "tensor",
        scatter_dimension=0,
        tiled=True,
    )


def body(*args):
    fits = (
        lax.axis_size("tensor") == 2 * LINE
        and args[0].shape[0] == BLOCK
        and args[4].shape[1] % 16 == 0
    )
    return (kernel_body if fits else plain_body)(*args)


def solution(mesh):
    in_specs = (
        P(("store", "tensor"), None),
        P(None, "tensor"),
        P(None, None, "tensor"),
        P("tensor", None),
        P("store", "tensor", None),
        P(),
        P(),
    )
    out_specs = P(("store", "tensor"), None)
    return jax.shard_map(body, mesh=mesh, in_specs=in_specs, out_specs=out_specs, check_vma=False)
```

```python
import functools
import math

import jax
import jax.numpy as jnp
from jax import lax
from jax.experimental import pallas as pl
from jax.experimental.pallas import tpu as pltpu
from jax.sharding import PartitionSpec as P

HD = 128
BLOCK = 64
NTOK = 128
NEIGH = 2
LINE = 4
F32 = jnp.float32
BF16 = jnp.bfloat16
MESH = pl.DeviceIdType.MESH


def main_kernel(
    store_count, capacity, requests,
    shard_ref, tile_ref, dec_ref, qw_hbm, kvw_hbm, ow_hbm, tiles_hbm, out_ref,
    rows, neigh, table, tiles, outgoing, arrived, qw, kvw, ow, q_buf, k_buf, v_buf, att,
    part, xrecv, up, down,
    load_sem, a2a_send, a2a_recv, rows_send, rows_recv, neigh_send, neigh_recv,
    part_send, part_recv, chain_send, up_recv, down_recv,
    edge_send, edge_recv, edge_x,
):
    store = lax.axis_index("store")
    tensor = lax.axis_index("tensor")
    z = lax.div(tensor, 2)
    x = lax.rem(tensor, 2)
    top = LINE - 1
    partner = z * 2 + 1 - x
    q_factor = 1.0 / math.sqrt(HD)
    head_count = qw.shape[1] // HD
    tile_rows = arrived.shape[1]
    width = rows.shape[2]
    cut = width * 11 // 16

    loads = [
        pltpu.make_async_copy(src, dst, load_sem.at[i])
        for i, (src, dst) in enumerate(
            ((tiles_hbm, tiles), (kvw_hbm, kvw), (qw_hbm, qw), (ow_hbm, ow))
        )
    ]
    own_slots = pl.ds(store * capacity, capacity)
    for load in loads:
        load.start()

    barrier = pltpu.get_barrier_semaphore()
    for k in range(1, store_count):
        peer = lax.rem(store + k, store_count)
        pl.semaphore_signal(barrier, inc=1, device_id=(peer, tensor), device_id_type=MESH)
    pl.semaphore_signal(barrier, inc=1, device_id=(store, partner), device_id_type=MESH)

    @pl.when(z > 0)
    def _():
        pl.semaphore_signal(barrier, inc=1, device_id=(store, tensor - 2), device_id_type=MESH)

    @pl.when(z < top)
    def _():
        pl.semaphore_signal(barrier, inc=1, device_id=(store, tensor + 2), device_id_type=MESH)

    @pl.loop(0, dec_ref.shape[0] // 16)
    def _(i):
        at = pl.ds(pl.multiple_of(i * 16, 16), 16)
        wide = dec_ref[at, :].astype(F32)
        scale = lax.rsqrt(jnp.mean(wide * wide, axis=1, keepdims=True) + 1e-05)
        rows[tensor, at, :] = (wide * scale).astype(BF16)

    inner = (z > 0) & (z < top)

    @pl.when(inner)
    def _():
        pl.semaphore_wait(barrier, store_count + 2)

    @pl.when(jnp.logical_not(inner))
    def _():
        pl.semaphore_wait(barrier, store_count + 1)

    def tiles_copy(k):
        peer = lax.rem(store + k, store_count)
        return pltpu.make_async_remote_copy(
            src_ref=outgoing.at[pl.ds(peer * capacity, capacity)],
            dst_ref=arrived.at[own_slots],
            send_sem=a2a_send.at[k - 1],
            recv_sem=a2a_recv.at[k - 1],
            device_id=(peer, tensor),
            device_id_type=MESH,
        )

    def block_copy(buf, columns, send, recv, way, j):
        target = (tensor + 2, tensor - 2, partner)[way]
        return pltpu.make_async_remote_copy(
            src_ref=buf.at[j, :, pl.ds(0, columns)],
            dst_ref=buf.at[j, :, pl.ds(0, columns)],
            send_sem=send.at[way, j],
            recv_sem=recv.at[j],
            device_id=(store, target),
            device_id_type=MESH,
        )

    row_copy = functools.partial(block_copy, rows, cut, rows_send, rows_recv)
    neigh_copy = functools.partial(block_copy, neigh, neigh.shape[2], neigh_send, neigh_recv)

    def edge_across(j):
        at = rows.at[j, :, pl.ds(cut, width - cut)]
        return pltpu.make_async_remote_copy(
            src_ref=at,
            dst_ref=at,
            send_sem=edge_x.at[0],
            recv_sem=edge_x.at[1],
            device_id=(store, partner),
            device_id_type=MESH,
        )

    def edge_copy(way, p):
        at = rows.at[pl.ds(p * 2, 2), :, pl.ds(cut, width - cut)]
        return pltpu.make_async_remote_copy(
            src_ref=at,
            dst_ref=at,
            send_sem=edge_send.at[way, p],
            recv_sem=edge_recv.at[p],
            device_id=(store, (tensor + 2, tensor - 2)[way]),
            device_id_type=MESH,
        )

    def send_own(copy):
        @pl.when(z < top)
        def _():
            copy(0, tensor).start()

        @pl.when(z > 0)
        def _():
            copy(1, tensor).start()

        copy(2, tensor).start()

    def forward(copy, d):
        @pl.when(z - d >= 0)
        def _():
            j = tensor - 2 * d
            copy(0, j).wait_recv()

            @pl.when(z < top)
            def _():
                copy(0, j).start()

            copy(2, j).start()

        @pl.when(z + d <= top)
        def _():
            j = tensor + 2 * d
            copy(1, j).wait_recv()

            @pl.when(z > 0)
            def _():
                copy(1, j).start()

            copy(2, j).start()

    edge_across(tensor).start()
    send_own(row_copy)

    for s in range(store_count):
        wanted = [jnp.int32(0)] * capacity
        seen = jnp.int32(0)
        for r in range(requests):
            n, b = r % NEIGH, (s * requests + r) // NEIGH
            hit = shard_ref[n, b] == store
            tile = tile_ref[n, b]
            for c in range(min(r + 1, capacity)):
                wanted[c] = jnp.where(hit & (seen == c), tile, wanted[c])
            seen = seen + hit.astype(jnp.int32)
        for c in range(capacity):
            table[s * capacity + c] = wanted[c]

    loads[0].wait()

    @pl.loop(0, store_count * capacity)
    def _(i):
        outgoing[i] = tiles[table[i]]

    for k in range(1, store_count):
        tiles_copy(k).start()

    for c in range(capacity):
        arrived[store * capacity + c] = outgoing[store * capacity + c]
    for k in range(1, store_count):
        tiles_copy(k).wait_recv()

    counts = [jnp.int32(0)] * store_count
    for r in range(requests):
        shard = shard_ref[r % NEIGH, store * (requests // NEIGH) + r // NEIGH]
        slot = shard * capacity
        for k in range(store_count):
            slot = slot + jnp.where(shard == k, counts[k], 0)
            counts[k] = counts[k] + (shard == k).astype(jnp.int32)
        neigh[tensor, pl.ds(r * tile_rows, tile_rows), :] = arrived[slot]

    send_own(neigh_copy)
    edge_across(partner).wait_recv()

    @pl.when(z < top)
    def _():
        edge_copy(0, z).start()

    @pl.when(z > 0)
    def _():
        edge_copy(1, z).start()

    def project(j):
        source = neigh[j]
        for a, dst in ((0, k_buf), (1, v_buf)):
            got = jnp.dot(source, kvw[a], preferred_element_type=F32).astype(BF16)
            dst[j] = got.reshape(dst.shape[1:])

    loads[1].wait()
    project(tensor)

    @pl.loop(1, LINE)
    def _(d):
        forward(row_copy, d)

        @pl.when(z - d >= 0)
        def _():
            edge_copy(0, z - d).wait_recv()

            @pl.when(z < top)
            def _():
                edge_copy(0, z - d).start()

        @pl.when(z + d <= top)
        def _():
            edge_copy(1, z + d).wait_recv()

            @pl.when(z > 0)
            def _():
                edge_copy(1, z + d).start()

        forward(neigh_copy, d)

        @pl.when(z - d >= 0)
        def _():
            project(tensor - 2 * d)

        @pl.when(z + d <= top)
        def _():
            project(tensor + 2 * d)

    for p in range(LINE):
        row_copy(2, p * 2 + 1 - x).wait_recv()
    loads[2].wait()

    @pl.loop(0, qw.shape[1] // 256)
    def _(c):
        at = pl.ds(pl.multiple_of(c * 256, 256), 256)
        all_rows = rows[...].reshape(-1, rows.shape[2])
        got = jnp.dot(all_rows, qw[:, at], preferred_element_type=F32)
        q_buf[:, :, at] = (got * q_factor).astype(BF16).reshape(q_buf.shape[0], BLOCK, 256)

    half = lax.div(z, 2)
    near = z + half * (3 - 2 * z)

    def place(k):
        o = (3, 2 - 2 * near, 1 + near, near)[k]
        return o + half * (3 - 2 * o)

    for k in reversed(range(LINE)):
        j = place(k) * 2 + 1 - x
        neigh_copy(2, j).wait_recv()
        project(j)
    loads[3].wait()

    def part_copy(p):
        return pltpu.make_async_remote_copy(
            src_ref=part.at[p, 1 - x],
            dst_ref=xrecv.at[p],
            send_sem=part_send.at[p],
            recv_sem=part_recv.at[p],
            device_id=(store, partner),
            device_id_type=MESH,
        )

    def chain_copy(way, p):
        return pltpu.make_async_remote_copy(
            src_ref=part.at[p, x],
            dst_ref=(up, down)[way].at[p],
            send_sem=chain_send.at[p],
            recv_sem=(up_recv, down_recv)[way].at[p],
            device_id=(store, (tensor + 2, tensor - 2)[way]),
            device_id_type=MESH,
        )

    def attend(p):
        @pl.loop(0, 2)
        def _(i):
            b = p * 2 + i
            for h in range(head_count):
                cols = slice(h * HD, (h + 1) * HD)
                keys = k_buf[:, b, :, cols].reshape(-1, HD)
                values = v_buf[:, b, :, cols].reshape(-1, HD)
                scores = lax.dot_general(
                    q_buf[b, :, cols], keys, (((1,), (1,)), ((), ())),
                    preferred_element_type=F32,
                )
                expo = jnp.exp(scores)
                weights = (expo / jnp.sum(expo, axis=1, keepdims=True)).astype(BF16)
                got = jnp.dot(weights, values, preferred_element_type=F32)
                att[i, :, cols] = got.astype(BF16)

        @pl.loop(0, ow.shape[1] // 512)
        def _(c):
            at = pl.ds(pl.multiple_of(c * 512, 512), 512)
            both = att[...].reshape(-1, att.shape[2])
            got = jnp.dot(both, ow[:, at], preferred_element_type=F32).astype(BF16)
            part[p, :, :, at] = got.reshape(2, BLOCK, 512)

        part_copy(p).start()

    def add(p, *terms):
        @pl.loop(0, BLOCK // 16)
        def _(i):
            at = pl.ds(pl.multiple_of(i * 16, 16), 16)
            total = part[p, x, at, :].astype(F32)
            for term in terms:
                total = total + term[p, at, :].astype(F32)
            part[p, x, at, :] = total.astype(BF16)

    def pass_on(p):
        part_copy(p).wait_recv()
        add(p, xrecv)

        @pl.when(p > z)
        def _():
            @pl.when(z > 0)
            def _():
                chain_copy(0, p).wait_recv()
                add(p, up)

            chain_copy(0, p).start()

        @pl.when(p < z)
        def _():
            @pl.when(z < top)
            def _():
                chain_copy(1, p).wait_recv()
                add(p, down)

            chain_copy(1, p).start()

    attend(place(0))
    attend(place(1))

    @pl.when(jnp.logical_not(inner))
    def _():
        pass_on(place(0))

    attend(place(2))
    attend(place(3))

    @pl.when(inner)
    def _():
        pass_on(place(0))

    pass_on(place(1))
    pass_on(place(2))
    part_copy(z).wait_recv()
    add(z, xrecv)

    @pl.when(z > 0)
    def _():
        chain_copy(0, z).wait_recv()
        add(z, up)

    @pl.when(z < top)
    def _():
        chain_copy(1, z).wait_recv()
        add(z, down)

    out_ref[...] = part[z, x]
    edge_across(tensor).wait_send()

    for k in range(1, store_count):
        tiles_copy(k).wait_send()
    for copy in (row_copy, neigh_copy):
        for p in range(LINE):
            j = p * 2 + x

            @pl.when((p <= z) & (z < top))
            def _():
                copy(0, j).wait_send()

            @pl.when((p >= z) & (z > 0))
            def _():
                copy(1, j).wait_send()

            copy(2, j).wait_send()
    for p in range(LINE):
        part_copy(p).wait_send()

        @pl.when(z != p)
        def _():
            chain_copy(0, p).wait_send()

        @pl.when((p <= z) & (z < top))
        def _():
            edge_copy(0, p).wait_send()

        @pl.when((p >= z) & (z > 0))
        def _():
            edge_copy(1, p).wait_send()


def kernel_body(
    decoder_rows, q_weight, kv_weight, out_weight, store_tiles, neighbour_shard, neighbour_tile
):
    tensor_count = lax.axis_size("tensor")
    store_count = lax.axis_size("store")
    local_rows, width = decoder_rows.shape
    blocks = tensor_count * local_rows // BLOCK
    requests = blocks * NEIGH
    capacity = 3 * requests // (2 * store_count)
    slots = store_count * capacity
    tile_rows, enc = store_tiles.shape[1:]
    head_cols = q_weight.shape[1]
    hbm = pl.BlockSpec(memory_space=pl.ANY)
    smem = pl.BlockSpec(memory_space=pltpu.SMEM)
    vmem = pl.BlockSpec(memory_space=pltpu.VMEM)
    dma = pltpu.SemaphoreType.DMA
    block_keys = NEIGH * tile_rows
    return pl.pallas_call(
        functools.partial(main_kernel, store_count, capacity, requests),
        out_shape=jax.ShapeDtypeStruct((local_rows, width), BF16),
        in_specs=[smem, smem, vmem, hbm, hbm, hbm, hbm],
        out_specs=vmem,
        scratch_shapes=[
            pltpu.VMEM((tensor_count, local_rows, width), BF16),
            pltpu.VMEM((tensor_count, requests * tile_rows, enc), BF16),
            pltpu.SMEM((slots,), jnp.int32),
            pltpu.VMEM(store_tiles.shape, BF16),
            pltpu.VMEM((slots, tile_rows, enc), BF16),
            pltpu.VMEM((slots, tile_rows, enc), BF16),
            pltpu.VMEM(q_weight.shape, BF16),
            pltpu.VMEM(kv_weight.shape, BF16),
            pltpu.VMEM(out_weight.shape, BF16),
            pltpu.VMEM((blocks, BLOCK, head_cols), BF16),
            pltpu.VMEM((tensor_count, blocks, block_keys, head_cols), BF16),
            pltpu.VMEM((tensor_count, blocks, block_keys, head_cols), BF16),
            pltpu.VMEM((2, BLOCK, head_cols), BF16),
            pltpu.VMEM((LINE, 2, BLOCK, width), BF16),
            pltpu.VMEM((LINE, BLOCK, width), BF16),
            pltpu.VMEM((LINE, BLOCK, width), BF16),
            pltpu.VMEM((LINE, BLOCK, width), BF16),
            dma((4,)),
            dma((store_count - 1,)),
            dma((store_count - 1,)),
            dma((3, tensor_count)),
            dma((tensor_count,)),
            dma((3, tensor_count)),
            dma((tensor_count,)),
            dma((LINE,)),
            dma((LINE,)),
            dma((LINE,)),
            dma((LINE,)),
            dma((LINE,)),
            dma((2, LINE)),
            dma((LINE,)),
            dma((2,)),
        ],
        compiler_params=pltpu.CompilerParams(
            collective_id=0, has_side_effects=True, vmem_limit_bytes=56 * 2**20
        ),
    )(
        neighbour_shard.T, neighbour_tile.T, decoder_rows, q_weight, kv_weight, out_weight,
        store_tiles,
    )


def plain_body(
    decoder_rows, q_weight, kv_weight, out_weight, store_tiles, neighbour_shard, neighbour_tile
):
    tensor_count = lax.axis_size("tensor")
    store_count = lax.axis_size("store")
    my_sequence = lax.axis_index("store")
    local_rows = decoder_rows.shape[0]
    seq_len = local_rows * tensor_count
    block_count = seq_len // BLOCK
    request_count = block_count * NEIGH
    capacity = 3 * request_count // (2 * store_count)
    head_cols = q_weight.shape[1]
    head_count = head_cols // HD
    q_factor = 1.0 / math.sqrt(HD)
    rows_wide = decoder_rows.astype(jnp.float32)
    normed = (
        rows_wide * lax.rsqrt(jnp.mean(rows_wide * rows_wide, axis=1, keepdims=True) + 1e-05)
    ).astype(jnp.bfloat16)
    queries = (
        jnp.dot(
            lax.all_gather(normed, "tensor", axis=0, tiled=True),
            q_weight,
            preferred_element_type=jnp.float32,
        )
        * q_factor
    ).astype(jnp.bfloat16)
    shard_table = neighbour_shard.reshape(store_count, request_count)
    tile_table = neighbour_tile.reshape(store_count, request_count)
    positions = jnp.arange(request_count, dtype=jnp.int32)
    before_mask = positions[None, :] < positions[:, None]
    same_shard = shard_table[:, :, None] == shard_table[:, None, :]
    rank_table = jnp.sum((same_shard & before_mask[None]).astype(jnp.int32), axis=2)
    served_here = shard_table == my_sequence
    slot_ids = jnp.arange(capacity, dtype=jnp.int32)
    slot_match = (
        served_here[:, :, None] & (rank_table[:, :, None] == slot_ids[None, None, :])
    ).astype(jnp.int32)
    slot_tile = jnp.sum(slot_match * tile_table[:, :, None], axis=1)
    outgoing = jnp.take(store_tiles, slot_tile.reshape(-1), axis=0)
    arrived = lax.all_to_all(outgoing, "store", split_axis=0, concat_axis=0, tiled=True)
    own_shard = lax.dynamic_index_in_dim(shard_table, my_sequence, 0, keepdims=False)
    own_rank = lax.dynamic_index_in_dim(rank_table, my_sequence, 0, keepdims=False)
    slot_index = own_shard * capacity + own_rank
    picked = jnp.take(arrived, slot_index, axis=0)
    projected = jnp.einsum(
        "rne,ced->rncd",
        lax.all_gather(picked, "tensor", axis=1, tiled=True),
        kv_weight,
        preferred_element_type=jnp.float32,
    )
    keys_values = projected.astype(jnp.bfloat16)
    keyed = keys_values.reshape(block_count, NEIGH * NTOK, 2, head_count, HD)
    query_blocks = queries.reshape(block_count, BLOCK, head_count, HD)
    scores = jnp.einsum(
        "cqhd,ckhd->chqk", query_blocks, keyed[:, :, 0], preferred_element_type=jnp.float32
    )
    expo_scores = jnp.exp(scores)
    weights = (expo_scores / jnp.sum(expo_scores, axis=3, keepdims=True)).astype(jnp.bfloat16)
    attended = jnp.einsum(
        "chqk,ckhd->cqhd", weights, keyed[:, :, 1], preferred_element_type=jnp.float32
    )
    attended = attended.astype(jnp.bfloat16).reshape(seq_len, head_cols)
    return lax.psum_scatter(
        jnp.dot(attended, out_weight, preferred_element_type=jnp.float32).astype(jnp.bfloat16),
        "tensor",
        scatter_dimension=0,
        tiled=True,
    )


def body(*args):
    fits = (
        lax.axis_size("tensor") == 2 * LINE
        and args[0].shape[0] == BLOCK
        and args[4].shape[1] % 16 == 0
    )
    return (kernel_body if fits else plain_body)(*args)


def solution(mesh):
    in_specs = (
        P(("store", "tensor"), None),
        P(None, "tensor"),
        P(None, None, "tensor"),
        P("tensor", None),
        P("store", "tensor", None),
        P(),
        P(),
    )
    out_specs = P(("store", "tensor"), None)
    return jax.shard_map(body, mesh=mesh, in_specs=in_specs, out_specs=out_specs, check_vma=False)
```

```python
import functools
import math

import jax
import jax.numpy as jnp
from jax import lax
from jax.experimental import pallas as pl
from jax.experimental.pallas import tpu as pltpu
from jax.sharding import PartitionSpec as P

HD = 128
BLOCK = 64
NTOK = 128
NEIGH = 2
LINE = 4
F32 = jnp.float32
BF16 = jnp.bfloat16
MESH = pl.DeviceIdType.MESH


def main_kernel(
    store_count, capacity, requests,
    shard_ref, tile_ref, dec_ref, qw_hbm, kvw_hbm, ow_hbm, tiles_hbm, out_ref,
    rows, neigh, table, tiles, outgoing, arrived, qw, kvw, ow, q_buf, k_buf, v_buf, att,
    part, xrecv, up, down, side_up, side_down, side_x,
    load_sem, a2a_send, a2a_recv, rows_send, rows_recv, neigh_send, neigh_recv,
    part_send, part_recv, chain_send, up_recv, down_recv,
    edge_send, edge_recv, edge_x, side_send, side_up_recv, side_down_recv, side_x_sem,
):
    store = lax.axis_index("store")
    tensor = lax.axis_index("tensor")
    z = lax.div(tensor, 2)
    x = lax.rem(tensor, 2)
    top = LINE - 1
    partner = z * 2 + 1 - x
    q_factor = 1.0 / math.sqrt(HD)
    head_count = qw.shape[1] // HD
    tile_rows = arrived.shape[1]
    width = rows.shape[2]
    cut = width * 11 // 16
    side = width * 13 // 16

    loads = [
        pltpu.make_async_copy(src, dst, load_sem.at[i])
        for i, (src, dst) in enumerate(
            ((tiles_hbm, tiles), (kvw_hbm, kvw), (qw_hbm, qw), (ow_hbm, ow))
        )
    ]
    own_slots = pl.ds(store * capacity, capacity)
    for load in loads:
        load.start()

    barrier = pltpu.get_barrier_semaphore()
    for k in range(1, store_count):
        peer = lax.rem(store + k, store_count)
        pl.semaphore_signal(barrier, inc=1, device_id=(peer, tensor), device_id_type=MESH)
    pl.semaphore_signal(barrier, inc=1, device_id=(store, partner), device_id_type=MESH)

    @pl.when(z > 0)
    def _():
        pl.semaphore_signal(barrier, inc=1, device_id=(store, tensor - 2), device_id_type=MESH)

    @pl.when(z < top)
    def _():
        pl.semaphore_signal(barrier, inc=1, device_id=(store, tensor + 2), device_id_type=MESH)

    @pl.loop(0, dec_ref.shape[0] // 16)
    def _(i):
        at = pl.ds(pl.multiple_of(i * 16, 16), 16)
        wide = dec_ref[at, :].astype(F32)
        scale = lax.rsqrt(jnp.mean(wide * wide, axis=1, keepdims=True) + 1e-05)
        rows[tensor, at, :] = (wide * scale).astype(BF16)

    inner = (z > 0) & (z < top)

    @pl.when(inner)
    def _():
        pl.semaphore_wait(barrier, store_count + 2)

    @pl.when(jnp.logical_not(inner))
    def _():
        pl.semaphore_wait(barrier, store_count + 1)

    def tiles_copy(k):
        peer = lax.rem(store + k, store_count)
        return pltpu.make_async_remote_copy(
            src_ref=outgoing.at[pl.ds(peer * capacity, capacity)],
            dst_ref=arrived.at[own_slots],
            send_sem=a2a_send.at[k - 1],
            recv_sem=a2a_recv.at[k - 1],
            device_id=(peer, tensor),
            device_id_type=MESH,
        )

    def block_copy(buf, columns, send, recv, way, j):
        target = (tensor + 2, tensor - 2, partner)[way]
        return pltpu.make_async_remote_copy(
            src_ref=buf.at[j, :, pl.ds(0, columns)],
            dst_ref=buf.at[j, :, pl.ds(0, columns)],
            send_sem=send.at[way, j],
            recv_sem=recv.at[j],
            device_id=(store, target),
            device_id_type=MESH,
        )

    row_copy = functools.partial(block_copy, rows, cut, rows_send, rows_recv)
    neigh_copy = functools.partial(block_copy, neigh, neigh.shape[2], neigh_send, neigh_recv)

    def edge_across(j):
        at = rows.at[j, :, pl.ds(cut, width - cut)]
        return pltpu.make_async_remote_copy(
            src_ref=at,
            dst_ref=at,
            send_sem=edge_x.at[0],
            recv_sem=edge_x.at[1],
            device_id=(store, partner),
            device_id_type=MESH,
        )

    def edge_copy(way, p):
        at = rows.at[pl.ds(p * 2, 2), :, pl.ds(cut, width - cut)]
        return pltpu.make_async_remote_copy(
            src_ref=at,
            dst_ref=at,
            send_sem=edge_send.at[way, p],
            recv_sem=edge_recv.at[p],
            device_id=(store, (tensor + 2, tensor - 2)[way]),
            device_id_type=MESH,
        )

    def send_own(copy):
        @pl.when(z < top)
        def _():
            copy(0, tensor).start()

        @pl.when(z > 0)
        def _():
            copy(1, tensor).start()

        copy(2, tensor).start()

    def forward(copy, d):
        @pl.when(z - d >= 0)
        def _():
            j = tensor - 2 * d
            copy(0, j).wait_recv()

            @pl.when(z < top)
            def _():
                copy(0, j).start()

            copy(2, j).start()

        @pl.when(z + d <= top)
        def _():
            j = tensor + 2 * d
            copy(1, j).wait_recv()

            @pl.when(z > 0)
            def _():
                copy(1, j).start()

            copy(2, j).start()

    edge_across(tensor).start()
    send_own(row_copy)

    for s in range(store_count):
        wanted = [jnp.int32(0)] * capacity
        seen = jnp.int32(0)
        for r in range(requests):
            n, b = r % NEIGH, (s * requests + r) // NEIGH
            hit = shard_ref[n, b] == store
            tile = tile_ref[n, b]
            for c in range(min(r + 1, capacity)):
                wanted[c] = jnp.where(hit & (seen == c), tile, wanted[c])
            seen = seen + hit.astype(jnp.int32)
        for c in range(capacity):
            table[s * capacity + c] = wanted[c]

    loads[0].wait()

    @pl.loop(0, store_count * capacity)
    def _(i):
        outgoing[i] = tiles[table[i]]

    for k in range(1, store_count):
        tiles_copy(k).start()

    for c in range(capacity):
        arrived[store * capacity + c] = outgoing[store * capacity + c]
    for k in range(1, store_count):
        tiles_copy(k).wait_recv()

    counts = [jnp.int32(0)] * store_count
    for r in range(requests):
        shard = shard_ref[r % NEIGH, store * (requests // NEIGH) + r // NEIGH]
        slot = shard * capacity
        for k in range(store_count):
            slot = slot + jnp.where(shard == k, counts[k], 0)
            counts[k] = counts[k] + (shard == k).astype(jnp.int32)
        neigh[tensor, pl.ds(r * tile_rows, tile_rows), :] = arrived[slot]

    send_own(neigh_copy)
    edge_across(partner).wait_recv()

    @pl.when(z < top)
    def _():
        edge_copy(0, z).start()

    @pl.when(z > 0)
    def _():
        edge_copy(1, z).start()

    def project(j):
        source = neigh[j]
        for a, dst in ((0, k_buf), (1, v_buf)):
            got = jnp.dot(source, kvw[a], preferred_element_type=F32).astype(BF16)
            dst[j] = got.reshape(dst.shape[1:])


    @pl.loop(1, LINE)
    def _(d):
        forward(row_copy, d)
        forward(neigh_copy, d)

        @pl.when(z - d >= 0)
        def _():
            edge_copy(0, z - d).wait_recv()

            @pl.when(z < top)
            def _():
                edge_copy(0, z - d).start()

        @pl.when(z + d <= top)
        def _():
            edge_copy(1, z + d).wait_recv()

            @pl.when(z > 0)
            def _():
                edge_copy(1, z + d).start()

    loads[1].wait()

    @pl.loop(0, LINE)
    def _(p):
        project(p * 2 + x)

    for p in range(LINE):
        row_copy(2, p * 2 + 1 - x).wait_recv()
    loads[2].wait()

    @pl.loop(0, qw.shape[1] // 256)
    def _(c):
        at = pl.ds(pl.multiple_of(c * 256, 256), 256)
        all_rows = rows[...].reshape(-1, rows.shape[2])
        got = jnp.dot(all_rows, qw[:, at], preferred_element_type=F32)
        q_buf[:, :, at] = (got * q_factor).astype(BF16).reshape(q_buf.shape[0], BLOCK, 256)

    half = lax.div(z, 2)
    near = z + half * (3 - 2 * z)

    def place(k):
        o = (3, 2 - 2 * near, 1 + near, near)[k]
        return o + half * (3 - 2 * o)

    for k in reversed(range(LINE)):
        j = place(k) * 2 + 1 - x
        neigh_copy(2, j).wait_recv()
        project(j)
    loads[3].wait()

    def part_copy(p):
        return pltpu.make_async_remote_copy(
            src_ref=part.at[p, 1 - x, :, pl.ds(0, side)],
            dst_ref=xrecv.at[p],
            send_sem=part_send.at[p],
            recv_sem=part_recv.at[p],
            device_id=(store, partner),
            device_id_type=MESH,
        )

    def chain_copy(way, p):
        return pltpu.make_async_remote_copy(
            src_ref=part.at[p, x, :, pl.ds(0, side)],
            dst_ref=(up, down)[way].at[p],
            send_sem=chain_send.at[p],
            recv_sem=(up_recv, down_recv)[way].at[p],
            device_id=(store, (tensor + 2, tensor - 2)[way]),
            device_id_type=MESH,
        )

    def side_copy(way, p):
        return pltpu.make_async_remote_copy(
            src_ref=part.at[p, :, :, pl.ds(side, width - side)],
            dst_ref=(side_up, side_down)[way].at[p],
            send_sem=side_send.at[p],
            recv_sem=(side_up_recv, side_down_recv)[way].at[p],
            device_id=(store, (tensor + 2, tensor - 2)[way]),
            device_id_type=MESH,
        )

    def side_across():
        return pltpu.make_async_remote_copy(
            src_ref=part.at[z, 1 - x, :, pl.ds(side, width - side)],
            dst_ref=side_x,
            send_sem=side_x_sem.at[0],
            recv_sem=side_x_sem.at[1],
            device_id=(store, partner),
            device_id_type=MESH,
        )

    def add_side(p, term):
        @pl.loop(0, 2 * BLOCK // 16)
        def _(i):
            c = lax.div(i, BLOCK // 16)
            at = pl.ds(pl.multiple_of(lax.rem(i, BLOCK // 16) * 16, 16), 16)
            total = part[p, c, at, side:].astype(F32) + term[p, c, at, :].astype(F32)
            part[p, c, at, side:] = total.astype(BF16)

    def pass_side(p):
        @pl.when(p > z)
        def _():
            @pl.when(z > 0)
            def _():
                side_copy(0, p).wait_recv()
                add_side(p, side_up)

            side_copy(0, p).start()

        @pl.when(p < z)
        def _():
            @pl.when(z < top)
            def _():
                side_copy(1, p).wait_recv()
                add_side(p, side_down)

            side_copy(1, p).start()

    def attend(p):
        @pl.loop(0, 2)
        def _(i):
            b = p * 2 + i
            for h in range(head_count):
                cols = slice(h * HD, (h + 1) * HD)
                keys = k_buf[:, b, :, cols].reshape(-1, HD)
                values = v_buf[:, b, :, cols].reshape(-1, HD)
                scores = lax.dot_general(
                    q_buf[b, :, cols], keys, (((1,), (1,)), ((), ())),
                    preferred_element_type=F32,
                )
                expo = jnp.exp(scores)
                weights = (expo / jnp.sum(expo, axis=1, keepdims=True)).astype(BF16)
                got = jnp.dot(weights, values, preferred_element_type=F32)
                att[i, :, cols] = got.astype(BF16)

        @pl.loop(0, ow.shape[1] // 512)
        def _(c):
            at = pl.ds(pl.multiple_of(c * 512, 512), 512)
            both = att[...].reshape(-1, att.shape[2])
            got = jnp.dot(both, ow[:, at], preferred_element_type=F32).astype(BF16)
            part[p, :, :, at] = got.reshape(2, BLOCK, 512)

        part_copy(p).start()

    def add(p, *terms):
        @pl.loop(0, BLOCK // 16)
        def _(i):
            at = pl.ds(pl.multiple_of(i * 16, 16), 16)
            total = part[p, x, at, :side].astype(F32)
            for term in terms:
                total = total + term[p, at, :].astype(F32)
            part[p, x, at, :side] = total.astype(BF16)

    def pass_on(p):
        part_copy(p).wait_recv()
        add(p, xrecv)

        @pl.when(p > z)
        def _():
            @pl.when(z > 0)
            def _():
                chain_copy(0, p).wait_recv()
                add(p, up)

            chain_copy(0, p).start()

        @pl.when(p < z)
        def _():
            @pl.when(z < top)
            def _():
                chain_copy(1, p).wait_recv()
                add(p, down)

            chain_copy(1, p).start()

    attend(place(0))
    attend(place(1))

    @pl.when(jnp.logical_not(inner))
    def _():
        pass_side(place(0))
        pass_on(place(0))

    attend(place(2))

    @pl.when(inner)
    def _():
        pass_side(place(0))

    attend(place(3))

    @pl.when(inner)
    def _():
        pass_on(place(0))

    pass_side(place(1))
    pass_on(place(1))
    pass_side(place(2))
    pass_on(place(2))
    @pl.when(z > 0)
    def _():
        side_copy(0, z).wait_recv()
        add_side(z, side_up)

    @pl.when(z < top)
    def _():
        side_copy(1, z).wait_recv()
        add_side(z, side_down)

    side_across().start()
    part_copy(z).wait_recv()
    add(z, xrecv)

    @pl.when(z > 0)
    def _():
        chain_copy(0, z).wait_recv()
        add(z, up)

    @pl.when(z < top)
    def _():
        chain_copy(1, z).wait_recv()
        add(z, down)

    out_ref[:, :side] = part[z, x, :, :side]
    side_across().wait_recv()
    last = part[z, x, :, side:].astype(F32) + side_x[...].astype(F32)
    out_ref[:, side:] = last.astype(BF16)
    side_across().wait_send()
    edge_across(tensor).wait_send()

    for k in range(1, store_count):
        tiles_copy(k).wait_send()
    for copy in (row_copy, neigh_copy):
        for p in range(LINE):
            j = p * 2 + x

            @pl.when((p <= z) & (z < top))
            def _():
                copy(0, j).wait_send()

            @pl.when((p >= z) & (z > 0))
            def _():
                copy(1, j).wait_send()

            copy(2, j).wait_send()
    for p in range(LINE):
        part_copy(p).wait_send()

        @pl.when(z != p)
        def _():
            chain_copy(0, p).wait_send()
            side_copy(0, p).wait_send()

        @pl.when((p <= z) & (z < top))
        def _():
            edge_copy(0, p).wait_send()

        @pl.when((p >= z) & (z > 0))
        def _():
            edge_copy(1, p).wait_send()


def kernel_body(
    decoder_rows, q_weight, kv_weight, out_weight, store_tiles, neighbour_shard, neighbour_tile
):
    tensor_count = lax.axis_size("tensor")
    store_count = lax.axis_size("store")
    local_rows, width = decoder_rows.shape
    blocks = tensor_count * local_rows // BLOCK
    requests = blocks * NEIGH
    capacity = 3 * requests // (2 * store_count)
    slots = store_count * capacity
    tile_rows, enc = store_tiles.shape[1:]
    head_cols = q_weight.shape[1]
    hbm = pl.BlockSpec(memory_space=pl.ANY)
    smem = pl.BlockSpec(memory_space=pltpu.SMEM)
    vmem = pl.BlockSpec(memory_space=pltpu.VMEM)
    dma = pltpu.SemaphoreType.DMA
    block_keys = NEIGH * tile_rows
    side = width * 13 // 16
    return pl.pallas_call(
        functools.partial(main_kernel, store_count, capacity, requests),
        out_shape=jax.ShapeDtypeStruct((local_rows, width), BF16),
        in_specs=[smem, smem, vmem, hbm, hbm, hbm, hbm],
        out_specs=vmem,
        scratch_shapes=[
            pltpu.VMEM((tensor_count, local_rows, width), BF16),
            pltpu.VMEM((tensor_count, requests * tile_rows, enc), BF16),
            pltpu.SMEM((slots,), jnp.int32),
            pltpu.VMEM(store_tiles.shape, BF16),
            pltpu.VMEM((slots, tile_rows, enc), BF16),
            pltpu.VMEM((slots, tile_rows, enc), BF16),
            pltpu.VMEM(q_weight.shape, BF16),
            pltpu.VMEM(kv_weight.shape, BF16),
            pltpu.VMEM(out_weight.shape, BF16),
            pltpu.VMEM((blocks, BLOCK, head_cols), BF16),
            pltpu.VMEM((tensor_count, blocks, block_keys, head_cols), BF16),
            pltpu.VMEM((tensor_count, blocks, block_keys, head_cols), BF16),
            pltpu.VMEM((2, BLOCK, head_cols), BF16),
            pltpu.VMEM((LINE, 2, BLOCK, width), BF16),
            pltpu.VMEM((LINE, BLOCK, side), BF16),
            pltpu.VMEM((LINE, BLOCK, side), BF16),
            pltpu.VMEM((LINE, BLOCK, side), BF16),
            pltpu.VMEM((LINE, 2, BLOCK, width - side), BF16),
            pltpu.VMEM((LINE, 2, BLOCK, width - side), BF16),
            pltpu.VMEM((BLOCK, width - side), BF16),
            dma((4,)),
            dma((store_count - 1,)),
            dma((store_count - 1,)),
            dma((3, tensor_count)),
            dma((tensor_count,)),
            dma((3, tensor_count)),
            dma((tensor_count,)),
            dma((LINE,)),
            dma((LINE,)),
            dma((LINE,)),
            dma((LINE,)),
            dma((LINE,)),
            dma((2, LINE)),
            dma((LINE,)),
            dma((2,)),
            dma((LINE,)),
            dma((LINE,)),
            dma((LINE,)),
            dma((2,)),
        ],
        compiler_params=pltpu.CompilerParams(
            collective_id=0, has_side_effects=True, vmem_limit_bytes=56 * 2**20
        ),
    )(
        neighbour_shard.T, neighbour_tile.T, decoder_rows, q_weight, kv_weight, out_weight,
        store_tiles,
    )


def plain_body(
    decoder_rows, q_weight, kv_weight, out_weight, store_tiles, neighbour_shard, neighbour_tile
):
    tensor_count = lax.axis_size("tensor")
    store_count = lax.axis_size("store")
    my_sequence = lax.axis_index("store")
    local_rows = decoder_rows.shape[0]
    seq_len = local_rows * tensor_count
    block_count = seq_len // BLOCK
    request_count = block_count * NEIGH
    capacity = 3 * request_count // (2 * store_count)
    head_cols = q_weight.shape[1]
    head_count = head_cols // HD
    q_factor = 1.0 / math.sqrt(HD)
    rows_wide = decoder_rows.astype(jnp.float32)
    normed = (
        rows_wide * lax.rsqrt(jnp.mean(rows_wide * rows_wide, axis=1, keepdims=True) + 1e-05)
    ).astype(jnp.bfloat16)
    queries = (
        jnp.dot(
            lax.all_gather(normed, "tensor", axis=0, tiled=True),
            q_weight,
            preferred_element_type=jnp.float32,
        )
        * q_factor
    ).astype(jnp.bfloat16)
    shard_table = neighbour_shard.reshape(store_count, request_count)
    tile_table = neighbour_tile.reshape(store_count, request_count)
    positions = jnp.arange(request_count, dtype=jnp.int32)
    before_mask = positions[None, :] < positions[:, None]
    same_shard = shard_table[:, :, None] == shard_table[:, None, :]
    rank_table = jnp.sum((same_shard & before_mask[None]).astype(jnp.int32), axis=2)
    served_here = shard_table == my_sequence
    slot_ids = jnp.arange(capacity, dtype=jnp.int32)
    slot_match = (
        served_here[:, :, None] & (rank_table[:, :, None] == slot_ids[None, None, :])
    ).astype(jnp.int32)
    slot_tile = jnp.sum(slot_match * tile_table[:, :, None], axis=1)
    outgoing = jnp.take(store_tiles, slot_tile.reshape(-1), axis=0)
    arrived = lax.all_to_all(outgoing, "store", split_axis=0, concat_axis=0, tiled=True)
    own_shard = lax.dynamic_index_in_dim(shard_table, my_sequence, 0, keepdims=False)
    own_rank = lax.dynamic_index_in_dim(rank_table, my_sequence, 0, keepdims=False)
    slot_index = own_shard * capacity + own_rank
    picked = jnp.take(arrived, slot_index, axis=0)
    projected = jnp.einsum(
        "rne,ced->rncd",
        lax.all_gather(picked, "tensor", axis=1, tiled=True),
        kv_weight,
        preferred_element_type=jnp.float32,
    )
    keys_values = projected.astype(jnp.bfloat16)
    keyed = keys_values.reshape(block_count, NEIGH * NTOK, 2, head_count, HD)
    query_blocks = queries.reshape(block_count, BLOCK, head_count, HD)
    scores = jnp.einsum(
        "cqhd,ckhd->chqk", query_blocks, keyed[:, :, 0], preferred_element_type=jnp.float32
    )
    expo_scores = jnp.exp(scores)
    weights = (expo_scores / jnp.sum(expo_scores, axis=3, keepdims=True)).astype(jnp.bfloat16)
    attended = jnp.einsum(
        "chqk,ckhd->cqhd", weights, keyed[:, :, 1], preferred_element_type=jnp.float32
    )
    attended = attended.astype(jnp.bfloat16).reshape(seq_len, head_cols)
    return lax.psum_scatter(
        jnp.dot(attended, out_weight, preferred_element_type=jnp.float32).astype(jnp.bfloat16),
        "tensor",
        scatter_dimension=0,
        tiled=True,
    )


def body(*args):
    fits = (
        lax.axis_size("tensor") == 2 * LINE
        and args[0].shape[0] == BLOCK
        and args[4].shape[1] % 16 == 0
    )
    return (kernel_body if fits else plain_body)(*args)


def solution(mesh):
    in_specs = (
        P(("store", "tensor"), None),
        P(None, "tensor"),
        P(None, None, "tensor"),
        P("tensor", None),
        P("store", "tensor", None),
        P(),
        P(),
    )
    out_specs = P(("store", "tensor"), None)
    return jax.shard_map(body, mesh=mesh, in_specs=in_specs, out_specs=out_specs, check_vma=False)
```
